512 devices in a mesh: dp: 64 (over z, y), seq: 8 (over x, core).
Axes of the slice: x: 4, y: 4, z: 16, core: 2. Of those that a mesh axis runs over, the one named last changes fastest.
Arguments:
- q_in: bfloat16 [65536, 3072], P(('dp', 'seq')), may hold values from -48 to 48
- k_in: bfloat16 [65536, 3072], P(('dp', 'seq')), may hold values from -48 to 48
- v_in: bfloat16 [65536, 3072], P(('dp', 'seq')), may hold values from -6 to 6
- gain_q: float32 [3072], P('dp'), may hold values from 0.5 to 2
- gain_k: float32 [3072], P('dp'), may hold values from 0.5 to 2
- clip_ids: int32 [64, 1024], P('dp'), may hold values from 0 to 3, never falling along the last dimension, each value on 1 to 512 neighbouring positions
Outputs:
- d_q: bfloat16 [65536, 3072], P(('dp', 'seq'))
- d_k: bfloat16 [65536, 3072], P(('dp', 'seq'))
- d_v: bfloat16 [65536, 3072], P(('dp', 'seq'))
- d_gain_q: float32 [3072], P('dp')
- d_gain_k: float32 [3072], P('dp')
The draws below stay inside these ranges and needn't reach their ends.
All inputs are finite; a program needn't handle non-finite values.
Results may differ from the reference program's by a relative error of at most 0.012.
The reference program's roundings to bfloat16 on the way (of `q_norm`, `probs_b`, `attn`, `dscore` and `dq_norm`) count: a program that leaves them out, or rounds other values in their place, can miss the bound.
Values may be sent and summed in bfloat16 or wider, within the bound.
No kernel may reach another device: no remote copies, remote signals or barrier semaphores. Data moves between devices by JAX's collectives and lax.ppermute only.
A program may use at most 64 MiB of HBM per device.

```python
import math
import jax
import jax.numpy as jnp
import numpy as np
from jax import lax

H = 24
HD = 128
TOK_DEV = 128
CLIPS = 4
G = 1024
CLIP_MAX = 512
TOKENS = 65536
N_DP = 64
N_SEQ = 8


def paired_rows(key, boost):
    width = H * HD
    base_q = jnp.clip(jax.random.normal(jax.random.fold_in(key, 101), (TOKENS, width), jnp.float32), -6.0, 6.0)
    base_k = jnp.clip(jax.random.normal(jax.random.fold_in(key, 102), (TOKENS, width), jnp.float32), -6.0, 6.0)
    rows = jnp.arange(TOKENS)[:, None]
    cols = jnp.arange(width)[None, :]
    chosen = rows % 37 == 0
    head_hit = cols // HD == rows % H
    keys_out = base_k * jnp.where(chosen & head_hit, boost, 1.0)
    queries = jnp.where(chosen & (boost > 1.0), keys_out, base_q)
    return (queries, keys_out)


def draw_q_in(key, part):
    boost = 1.0
    pair = paired_rows(key, boost)
    return pair[0].astype(jnp.bfloat16)


def draw_k_in(key, part):
    boost = 1.0
    pair = paired_rows(key, boost)
    return pair[1].astype(jnp.bfloat16)


def block_scale(own_key, shape, split, smallest, high):
    factor_of = 1.0
    for axis_at, parts in split:
        heights = jax.random.uniform(jax.random.fold_in(jax.random.fold_in(own_key, 6), axis_at), (parts,), jnp.float32, smallest / len(split), high / len(split))
        factor_of = factor_of * jnp.repeat(jnp.exp(heights), shape[axis_at] // parts).reshape((-1,) + (1,) * (len(shape) - 1 - axis_at))
    return factor_of


def length_profile(amount, total, most, skew):
    loads = [(1 << 20) // math.isqrt(rank ** skew) + 1 for rank in range(2, amount + 1)]
    rest, holding = total - most - (amount - 1), [1] * (amount - 1)
    while rest > 0:
        free = [i for i in range(amount - 1) if holding[i] < most]
        whole, left = sum([loads[i] for i in free]), rest
        for i in free:
            more = min(most - holding[i], max(1, left * loads[i] // whole), rest)
            holding[i] = holding[i] + more
            rest = rest - more
    return np.array([most] + holding)


def ragged_sizes(own_key, amount, total, most, slope):
    if amount == 2:
        one = jax.random.randint(own_key, (), max(1, total - most), min(most, total - 1) + 1)
        return jnp.stack([one, total - one])
    lengths = jnp.asarray(length_profile(amount, total, most, slope), jnp.int32)
    pairs = (amount - 1) // 2
    source_of, sink = lengths[1:1 + 2 * pairs:2], lengths[2:2 + 2 * pairs:2]
    slack = jnp.minimum(source_of - 1, most - sink)
    shifted = jax.random.randint(jax.random.fold_in(own_key, 1), (pairs,), 0, 1 << 20) % (slack + 1)
    lengths = lengths.at[1:1 + 2 * pairs:2].set(source_of - shifted).at[2:2 + 2 * pairs:2].set(sink + shifted)
    return lengths[jax.random.permutation(jax.random.fold_in(own_key, 2), amount)]


def centred(own_key, shape, scale, reach, pieces=(), kind=jnp.bfloat16):
    level = block_scale(own_key, shape, pieces, -0.22, 0.18) if pieces else 1.0
    array = jax.random.normal(own_key, shape, jnp.float32) * scale * level
    return jnp.minimum(jnp.maximum(array, -reach), reach).astype(kind)


def setup_inputs(seed: int = 0) -> dict:
    splits = jax.random.split(jax.random.key(seed), 7)
    return {
        "q_in": draw_q_in(jax.random.fold_in(splits[6], 71), 0),
        "k_in": draw_k_in(jax.random.fold_in(splits[6], 71), 0),
        "v_in": centred(splits[2], (TOKENS, H * HD), 1.0, 6.0, ((0, 512),)),
        "gain_q": jnp.clip(jnp.exp(math.log(2.0) - 1.3862944 * jax.random.uniform(splits[3], (H * HD,), jnp.float32) ** block_scale(splits[3], (H * HD,), ((0, 64),), -0.2, 0.2)), 0.5, 2.0),
        "gain_k": jnp.clip(jnp.exp(math.log(2.0) - 1.3862944 * jax.random.uniform(splits[4], (H * HD,), jnp.float32) ** block_scale(splits[4], (H * HD,), ((0, 64),), -0.2, 0.2)), 0.5, 2.0),
        "clip_ids": jax.vmap(lambda own: jnp.searchsorted(jnp.cumsum(ragged_sizes(own, CLIPS, TOK_DEV * N_SEQ, CLIP_MAX, 2)), jnp.arange(TOK_DEV * N_SEQ), side="right"))(jax.random.split(splits[5], N_DP)).reshape((N_DP, TOK_DEV * N_SEQ)).astype(jnp.int32),
    }


EPS = 1e-06

def normalize(x, gain):
    xf = x.astype(jnp.float32)
    inv = lax.rsqrt(lax.optimization_barrier(jnp.mean(xf * xf, axis=1, keepdims=True)) + EPS)
    hat = xf * inv
    return ((hat * gain).astype(jnp.bfloat16), inv, hat)

def head_grads(args):
    qh, kh, vh, same = args
    scale = HD ** (-0.5)
    scores = jnp.dot(qh, kh.T, preferred_element_type=jnp.float32) * scale
    scores = jnp.where(same, scores, -1e+30)
    top = lax.optimization_barrier(jnp.max(scores, axis=1, keepdims=True))
    expo = jnp.where(same, jnp.exp(scores - top), 0.0)
    probs = expo / lax.optimization_barrier(jnp.sum(expo, axis=1, keepdims=True))
    probs_b = probs.astype(jnp.bfloat16)
    attn = jnp.dot(probs_b, vh, preferred_element_type=jnp.float32).astype(jnp.bfloat16)
    grad_v = jnp.dot(probs_b.T, attn, preferred_element_type=jnp.float32).astype(jnp.bfloat16)
    dprobs = jnp.dot(attn, vh.T, preferred_element_type=jnp.float32)
    delta = lax.optimization_barrier(jnp.sum(probs * dprobs, axis=1, keepdims=True))
    dscore = (probs * (dprobs - delta) * scale).astype(jnp.bfloat16)
    grad_q = jnp.dot(dscore, kh, preferred_element_type=jnp.float32).astype(jnp.bfloat16)
    grad_k = jnp.dot(dscore.T, qh, preferred_element_type=jnp.float32).astype(jnp.bfloat16)
    return (grad_q, grad_k, grad_v)

def group_grads(args):
    qg, kg, vg, ids = args
    same = ids[:, None] == ids[None, :]
    qt = jnp.transpose(qg.reshape(G, H, HD), (1, 0, 2))
    kt = jnp.transpose(kg.reshape(G, H, HD), (1, 0, 2))
    vt = jnp.transpose(vg.reshape(G, H, HD), (1, 0, 2))

    def per_head(trio):
        return head_grads((trio[0], trio[1], trio[2], same))
    grad_q, grad_k, grad_v = lax.map(per_head, (qt, kt, vt))
    back = lambda a: jnp.transpose(a, (1, 0, 2)).reshape(G, H * HD)
    return (back(grad_q), back(grad_k), back(grad_v))

def norm_back(dnorm, gain, inv, hat):
    df = dnorm.astype(jnp.float32)
    dhat = df * gain
    grad = inv * (dhat - hat * lax.optimization_barrier(jnp.mean(dhat * hat, axis=1, keepdims=True)))
    return (grad.astype(jnp.bfloat16), lax.optimization_barrier(jnp.sum(df * hat, axis=0)))

def reference(q_in, k_in, v_in, gain_q, gain_k, clip_ids):
    q_norm, inv_q, hat_q = normalize(q_in, gain_q)
    k_norm, inv_k, hat_k = normalize(k_in, gain_k)
    width = H * HD
    qg = q_norm.reshape(N_DP, G, width)
    kg = k_norm.reshape(N_DP, G, width)
    vg = v_in.reshape(N_DP, G, width)
    dq_norm, dk_norm, grad_v = lax.map(group_grads, (qg, kg, vg, clip_ids))
    dq_norm = dq_norm.reshape(TOKENS, width)
    dk_norm = dk_norm.reshape(TOKENS, width)
    grad_v = grad_v.reshape(TOKENS, width)
    d_q, d_gain_q = norm_back(dq_norm, gain_q, inv_q, hat_q)
    d_k, d_gain_k = norm_back(dk_norm, gain_k, inv_k, hat_k)
    return (d_q, d_k, grad_v, d_gain_q, d_gain_k)
```

```python
import jax
import jax.numpy as jnp
from jax import lax
from jax.experimental import pallas as pl
from jax.experimental.pallas import tpu as pltpu
from jax.sharding import PartitionSpec as P

H = 24
HD = 128
TOK = 128
N_SEQ = 8
HEADS = H // N_SEQ
G = TOK * N_SEQ
WIDTH = H * HD
BQ = 256
EXTRA = 16
ROWS = 3 * TOK + EXTRA
EPS = 1e-06
SCALE = HD ** (-0.5)
LOG2E = 1.4426950408889634
SHARD = 48


def split3(x):
    hi = x.astype(jnp.bfloat16).astype(jnp.float32)
    mid = (x - hi).astype(jnp.bfloat16).astype(jnp.float32)
    return (hi, mid, x - hi - mid)


def extra_rows(row_a, row_b):
    at = lax.broadcasted_iota(jnp.int32, (EXTRA, HD), 0)
    out = jnp.zeros((EXTRA, HD), jnp.float32)
    for index, piece in enumerate(split3(row_a) + split3(row_b)):
        out = jnp.where(at == index, piece, out)
    return out.astype(jnp.bfloat16)


def join3(extra):
    x = extra.astype(jnp.float32)
    return ((x[0:1] + x[1:2]) + x[2:3], (x[3:4] + x[4:5]) + x[5:6])


def column(row):
    return jnp.transpose(jnp.broadcast_to(row, (HD, HD)))


def pack_kernel(q_ref, k_ref, v_ref, *outs):
    pays, inv_refs = outs[:HEADS], outs[HEADS:]
    rows = []
    for ref, inv_ref in zip((q_ref, k_ref), inv_refs):
        total = jnp.zeros((TOK, HD), jnp.float32)
        for h in range(H):
            x = ref[:, h * HD:(h + 1) * HD].astype(jnp.float32)
            total = total + x * x
        inv = lax.rsqrt(jnp.sum(total, axis=1, keepdims=True) * (1.0 / WIDTH) + EPS)
        inv = jnp.broadcast_to(inv, (TOK, HD))
        inv_ref[...] = inv
        rows.append(jnp.transpose(inv)[0:1])
    extra = extra_rows(rows[0], rows[1])
    for c in range(HEADS):
        for s in range(N_SEQ):
            h = s * HEADS + c
            for n, ref in enumerate((q_ref, k_ref, v_ref)):
                pays[c][s, n * TOK:(n + 1) * TOK] = ref[:, h * HD:(h + 1) * HD]
            pays[c][s, 3 * TOK:] = extra


def nt(a, b):
    return lax.dot_general(a, b, (((1,), (1,)), ((), ())), preferred_element_type=jnp.float32)


def nn(a, b):
    return jnp.dot(a, b, preferred_element_type=jnp.float32)


def attend_kernel(pay_ref, gain_ref, ids_ref, out_ref, dg_ref, qn, kn, vv, dq, acc_k, acc_v):
    gq, gk = gain_ref[0:1], gain_ref[1:2]

    def hats(j):
        iq, ik = join3(pay_ref[j, 3 * TOK:])
        q = pay_ref[j, 0:TOK].astype(jnp.float32) * column(iq)
        k = pay_ref[j, TOK:2 * TOK].astype(jnp.float32) * column(ik)
        return (q, k)

    for j in range(N_SEQ):
        q, k = hats(j)
        at = slice(j * TOK, (j + 1) * TOK)
        qn[at] = (q * gq).astype(jnp.bfloat16)
        kn[at] = (k * gk).astype(jnp.bfloat16)
        vv[at] = pay_ref[j, 2 * TOK:3 * TOK]
    acc_k[...] = jnp.zeros_like(acc_k)
    acc_v[...] = jnp.zeros_like(acc_v)
    ids = ids_ref[...]

    for b in range(G // BQ):
        at = slice(b * BQ, (b + 1) * BQ)
        same = jnp.concatenate(
            [column(ids[:, t:t + HD]) for t in range(b * BQ, (b + 1) * BQ, HD)], axis=0)[:, 0:1] == ids
        qb = qn[at]
        s = jnp.where(same, nt(qb, kn[...]), -1e30)
        top = jnp.max(s, axis=1, keepdims=True)
        e = jnp.exp2((s - top) * (SCALE * LOG2E))
        p = e * (1.0 / jnp.sum(e, axis=1, keepdims=True))
        pb = p.astype(jnp.bfloat16)
        attn = nn(pb, vv[...])
        attn_b = attn.astype(jnp.bfloat16)
        dp = nt(attn_b, vv[...])
        delta = jnp.sum(p * dp, axis=1, keepdims=True)
        ds = (p * (dp - delta) * SCALE).astype(jnp.bfloat16)
        dq[at] = nn(ds, kn[...]).astype(jnp.bfloat16)
        acc_v[...] += nn(jnp.transpose(attn_b), pb)
        acc_k[...] += nn(jnp.transpose(qb), ds)

    sum_q = jnp.zeros((1, HD), jnp.float32)
    sum_k = jnp.zeros((1, HD), jnp.float32)
    extra = extra_rows(gq, gk)
    for j in range(N_SEQ):
        at = slice(j * TOK, (j + 1) * TOK)
        q, k = hats(j)
        one_q = dq[at]
        one_k = jnp.transpose(acc_k[:, at]).astype(jnp.bfloat16)
        sum_q = sum_q + jnp.sum(one_q.astype(jnp.float32) * q, axis=0, keepdims=True)
        sum_k = sum_k + jnp.sum(one_k.astype(jnp.float32) * k, axis=0, keepdims=True)
        out_ref[j, 0:TOK] = one_q
        out_ref[j, TOK:2 * TOK] = one_k
        out_ref[j, 2 * TOK:3 * TOK] = jnp.transpose(acc_v[:, at]).astype(jnp.bfloat16)
        out_ref[j, 3 * TOK:] = extra
    dg_ref[0:1] = sum_q
    dg_ref[1:2] = sum_k


def final_kernel(q_ref, k_ref, inv_q_ref, inv_k_ref, *refs):
    pays, (dq_ref, dk_ref, dv_ref) = refs[:HEADS], refs[HEADS:]
    pairs = [(s, c, s * HEADS + c) for s in range(N_SEQ) for c in range(HEADS)]
    for n, (ref, inv_ref, out_ref) in enumerate(
            ((q_ref, inv_q_ref, dq_ref), (k_ref, inv_k_ref, dk_ref))):
        inv = inv_ref[...]

        def parts(s, c, h):
            gain = join3(pays[c][s, 3 * TOK:])[n]
            dhat = pays[c][s, n * TOK:(n + 1) * TOK].astype(jnp.float32) * gain
            return (dhat, ref[:, h * HD:(h + 1) * HD].astype(jnp.float32) * inv)

        total = jnp.zeros((TOK, HD), jnp.float32)
        for s, c, h in pairs:
            dhat, hat = parts(s, c, h)
            total = total + dhat * hat
        mean = jnp.sum(total, axis=1, keepdims=True) * (1.0 / WIDTH)
        for s, c, h in pairs:
            dhat, hat = parts(s, c, h)
            out_ref[:, h * HD:(h + 1) * HD] = (inv * (dhat - hat * mean)).astype(jnp.bfloat16)
    for s, c, h in pairs:
        dv_ref[:, h * HD:(h + 1) * HD] = pays[c][s, 2 * TOK:3 * TOK]


def shape(dims, dtype=jnp.bfloat16):
    return jax.ShapeDtypeStruct(dims, dtype)


PARAMS = pltpu.CompilerParams(vmem_limit_bytes=48 * 1024 * 1024)


def local(q_in, k_in, v_in, gain_q, gain_k, clip_ids):
    n_dp = lax.axis_size("dp")
    blocks = [list(range(b, b + N_SEQ)) for b in range(0, n_dp, N_SEQ)]
    swap = [((b * 8 + i) * 8 + s, (s * 8 + i) * 8 + b) for b in range(8) for i in range(8) for s in range(8)]

    gain = lax.ppermute(jnp.stack([gain_q, gain_k]), ("dp", "seq"), swap)
    gain = lax.all_to_all(jnp.broadcast_to(gain, (N_SEQ, 2, SHARD)), "dp", 0, 0,
                          axis_index_groups=blocks, tiled=True)
    gain = jnp.transpose(gain, (1, 0, 2)).reshape(2, HEADS * HD)

    pay = shape((N_SEQ, ROWS, HD))
    inv = shape((TOK, HD), jnp.float32)
    *pays, inv_q, inv_k = pl.pallas_call(
        pack_kernel, out_shape=[pay] * HEADS + [inv] * 2, compiler_params=PARAMS, name="pack",
    )(q_in, k_in, v_in)

    backs, sums = [], []
    for c in range(HEADS):
        got = lax.all_to_all(pays[c], "seq", 0, 0, tiled=True)
        back, dg = pl.pallas_call(
            attend_kernel,
            out_shape=[pay, shape((2, HD), jnp.float32)],
            scratch_shapes=[pltpu.VMEM((G, HD), jnp.bfloat16)] * 4 + [pltpu.VMEM((HD, G), jnp.float32)] * 2,
            compiler_params=PARAMS, name="attend",
            cost_estimate=pl.CostEstimate(flops=12 * G * G * HD, bytes_accessed=1600000, transcendentals=G * G),
        )(got, gain[:, c * HD:(c + 1) * HD], clip_ids)
        backs.append(lax.all_to_all(back, "seq", 0, 0, tiled=True))
        sums.append(dg)

    part = jnp.transpose(jnp.concatenate(sums, axis=1).reshape(2, N_SEQ, SHARD), (1, 0, 2))
    part = jnp.sum(lax.all_to_all(part, "dp", 0, 0, axis_index_groups=blocks, tiled=True), axis=0)
    part = lax.ppermute(part, ("dp", "seq"), swap)
    part = jnp.sum(lax.all_to_all(jnp.broadcast_to(part, (N_SEQ, 2, SHARD)), "seq", 0, 0, tiled=True), axis=0)

    out = shape((TOK, WIDTH))
    d_q, d_k, d_v = pl.pallas_call(
        final_kernel, out_shape=[out] * 3, compiler_params=PARAMS, name="final",
    )(q_in, k_in, inv_q, inv_k, *backs)
    return (d_q, d_k, d_v, part[0], part[1])


def solution(mesh):
    rows = P(("dp", "seq"), None)
    return jax.shard_map(
        local, mesh=mesh,
        in_specs=(rows, rows, rows, P("dp"), P("dp"), P("dp", None)),
        out_specs=(rows, rows, rows, P("dp"), P("dp")), check_vma=False)
```

```python
import jax
import jax.numpy as jnp
from jax import lax
from jax.experimental import pallas as pl
from jax.experimental.pallas import tpu as pltpu
from jax.sharding import PartitionSpec as P

H = 24
HD = 128
TOK = 128
N_SEQ = 8
HEADS = H // N_SEQ
G = TOK * N_SEQ
WIDTH = H * HD
BQ = 256
WINDOWS = (512, 640, 768, 1024)
EXTRA = 16
BODY = 3 * TOK * HEADS
EPS = 1e-06
SCALE = HD ** (-0.5)
LOG2E = 1.4426950408889634
SHARD = 48


def split3(x):
    hi = x.astype(jnp.bfloat16).astype(jnp.float32)
    mid = (x - hi).astype(jnp.bfloat16).astype(jnp.float32)
    return (hi, mid, x - hi - mid)


def extra_rows(rows, size):
    at = lax.broadcasted_iota(jnp.int32, (size, HD), 0)
    out = jnp.zeros((size, HD), jnp.float32)
    for index, piece in enumerate([piece for row in rows for piece in split3(row)]):
        out = jnp.where(at == index, piece, out)
    return out.astype(jnp.bfloat16)


def join3(extra, n):
    x = extra[3 * n:3 * n + 3]
    return (x[0:1] + x[1:2]) + x[2:3]


def column(row):
    return jnp.transpose(jnp.broadcast_to(row, (HD, HD)))


def body(c, n):
    return slice((c * 3 + n) * TOK, (c * 3 + n + 1) * TOK)


def pack_kernel(q_ref, k_ref, v_ref, pay_ref, inv_q_ref, inv_k_ref, mark_ref, held, extra, sems):
    loads = []
    for n, ref in enumerate((q_ref, k_ref)):
        loads.append(pltpu.make_async_copy(ref, held.at[n], sems.at[n]))
        loads[n].start()
    copies = []
    for s in range(N_SEQ):
        for c in range(HEADS):
            h = s * HEADS + c
            for n, ref in enumerate((q_ref, k_ref, v_ref)):
                copies.append(pltpu.make_async_copy(
                    ref.at[:, h * HD:(h + 1) * HD], pay_ref.at[s, body(c, n)], sems.at[2 + len(copies)]))
                copies[-1].start()
    rows = []
    for n, inv_ref in enumerate((inv_q_ref, inv_k_ref)):
        loads[n].wait()
        total = jnp.zeros((TOK, HD), jnp.float32)
        for h in range(H):
            x = held[n, :, h * HD:(h + 1) * HD].astype(jnp.float32)
            total = total + x * x
        inv = lax.rsqrt(jnp.sum(total, axis=1, keepdims=True) * (1.0 / WIDTH) + EPS)
        inv = jnp.broadcast_to(inv, (TOK, HD))
        inv_ref[...] = inv
        rows.append(jnp.transpose(inv)[0:1])
    mark_ref[...] = jnp.zeros_like(mark_ref)
    extra[...] = extra_rows(rows, EXTRA)
    for s in range(N_SEQ):
        copies.append(pltpu.make_async_copy(extra, pay_ref.at[s, BODY:], sems.at[2 + len(copies)]))
        copies[-1].start()
    for copy in copies:
        copy.wait()


def nt(a, b):
    return lax.dot_general(a, b, (((1,), (1,)), ((), ())), preferred_element_type=jnp.float32)


def nn(a, b):
    return jnp.dot(a, b, preferred_element_type=jnp.float32)


def attend_kernel(lo_ref, hi_ref, pay_ref, gain_ref, ids_ref, out_ref, dg_ref,
                  qn, kn, vv, dq, acc_k, acc_v, mq, mk, outs, sems):
    for j in range(N_SEQ):
        extra = pay_ref[j, BODY:].astype(jnp.float32)
        at = slice(j * TOK, (j + 1) * TOK)
        mq[at] = column(join3(extra, 0))
        mk[at] = column(join3(extra, 1))
    gains = [[gain_ref[n:n + 1, c * HD:(c + 1) * HD] for n in range(2)] for c in range(HEADS)]
    extra = extra_rows([row for pair in gains for row in pair], 2 * EXTRA)
    for j in range(N_SEQ):
        outs[j, BODY:] = extra

    def hats(c, j):
        at = slice(j * TOK, (j + 1) * TOK)
        return (pay_ref[j, body(c, 0)].astype(jnp.float32) * mq[at],
                pay_ref[j, body(c, 1)].astype(jnp.float32) * mk[at])

    for c in range(HEADS):
        for j in range(N_SEQ):
            q, k = hats(c, j)
            at = slice(j * TOK, (j + 1) * TOK)
            qn[c, at] = (q * gains[c][0]).astype(jnp.bfloat16)
            kn[c, at] = (k * gains[c][1]).astype(jnp.bfloat16)
            vv[c, at] = pay_ref[j, body(c, 2)]
    acc_k[...] = jnp.zeros_like(acc_k)
    acc_v[...] = jnp.zeros_like(acc_v)

    def block(b, first, width):
        first = pl.multiple_of(first, TOK)
        rows = pl.ds(pl.multiple_of(b * BQ, BQ), BQ)
        keys = pl.ds(first, width)
        own = [column(ids_ref[:, pl.ds(pl.multiple_of(b * BQ + t, HD), HD)])[:, 0:1] for t in range(0, BQ, HD)]
        same = jnp.concatenate(own, axis=0) == ids_ref[:, keys]
        for c in range(HEADS):
            qb, kb, vb = qn[c, rows], kn[c, keys], vv[c, keys]
            s = jnp.where(same, nt(qb, kb), -1e30)
            top = jnp.max(s, axis=1, keepdims=True)
            e = jnp.exp2((s - top) * (SCALE * LOG2E))
            p = e * (1.0 / jnp.sum(e, axis=1, keepdims=True))
            pb = p.astype(jnp.bfloat16)
            attn = nn(pb, vb).astype(jnp.bfloat16)
            dp = nt(attn, vb)
            delta = jnp.sum(p * dp, axis=1, keepdims=True)
            ds = (p * (dp - delta) * SCALE).astype(jnp.bfloat16)
            dq[c, rows] = nn(ds, kb).astype(jnp.bfloat16)
            acc_v[c, :, keys] += nn(jnp.transpose(attn), pb)
            acc_k[c, :, keys] += nn(jnp.transpose(qb), ds)

    def step(b, carry):
        low = lo_ref[b] // TOK * TOK
        span = hi_ref[b] - low
        done = None
        for width in WINDOWS:
            fits = span <= width
            now = fits if done is None else jnp.logical_and(fits, jnp.logical_not(done))
            done = fits

            @pl.when(now)
            def _():
                block(b, jnp.minimum(low, G - width), width)
        return carry

    lax.fori_loop(0, G // BQ, step, 0)

    copies = []
    for j in range(N_SEQ):
        at = slice(j * TOK, (j + 1) * TOK)
        for c in range(HEADS):
            outs[j, body(c, 0)] = dq[c, at]
            outs[j, body(c, 1)] = jnp.transpose(acc_k[c, :, at]).astype(jnp.bfloat16)
            outs[j, body(c, 2)] = jnp.transpose(acc_v[c, :, at]).astype(jnp.bfloat16)
        copies.append(pltpu.make_async_copy(outs.at[j], out_ref.at[j], sems.at[j]))
        copies[j].start()
    for c in range(HEADS):
        sums = [jnp.zeros((1, HD), jnp.float32)] * 2
        for j in range(N_SEQ):
            hat = hats(c, j)
            sums = [sums[n] + jnp.sum(outs[j, body(c, n)].astype(jnp.float32) * hat[n], axis=0, keepdims=True)
                    for n in range(2)]
        for n in range(2):
            dg_ref[n:n + 1, c * HD:(c + 1) * HD] = sums[n]
    for copy in copies:
        copy.wait()


def final_kernel(q_ref, k_ref, inv_q_ref, inv_k_ref, pay_ref, dq_ref, dk_ref, dv_ref):
    pairs = [(s, c, slice((s * HEADS + c) * HD, (s * HEADS + c + 1) * HD))
             for s in range(N_SEQ) for c in range(HEADS)]
    extras = [pay_ref[s, BODY:].astype(jnp.float32) for s in range(N_SEQ)]
    for n, (ref, inv_ref, out_ref) in enumerate(
            ((q_ref, inv_q_ref, dq_ref), (k_ref, inv_k_ref, dk_ref))):
        inv = inv_ref[...]

        def parts(s, c, cols):
            dhat = pay_ref[s, body(c, n)].astype(jnp.float32) * join3(extras[s], 2 * c + n)
            return (dhat, ref[:, cols].astype(jnp.float32) * inv)

        total = jnp.zeros((TOK, HD), jnp.float32)
        for pair in pairs:
            dhat, hat = parts(*pair)
            total = total + dhat * hat
        mean = jnp.sum(total, axis=1, keepdims=True) * (1.0 / WIDTH)
        for pair in pairs:
            dhat, hat = parts(*pair)
            out_ref[:, pair[2]] = (inv * (dhat - hat * mean)).astype(jnp.bfloat16)
    for s, c, cols in pairs:
        dv_ref[:, cols] = pay_ref[s, body(c, 2)]


def hold_kernel(x_ref, after_ref, out_ref):
    out_ref[...] = x_ref[...]


def hold(x, after):
    return pl.pallas_call(
        hold_kernel, out_shape=shape(x.shape, jnp.float32),
        in_specs=[pl.BlockSpec(memory_space=pltpu.VMEM), pl.BlockSpec(memory_space=pl.ANY)],
        name="hold", cost_estimate=pl.CostEstimate(flops=1 << 36, bytes_accessed=1 << 27, transcendentals=0),
    )(x, after)


def shape(dims, dtype=jnp.bfloat16):
    return jax.ShapeDtypeStruct(dims, dtype)


PARAMS = pltpu.CompilerParams(vmem_limit_bytes=48 * 1024 * 1024)


def swapped():
    return [((b * 8 + i) * 8 + s, (s * 8 + i) * 8 + b) for b in range(8) for i in range(8) for s in range(8)]


def sum_four(x, axis, pairs):
    one, two, three = (lax.ppermute(x, axis, pairs(k)) for k in (1, 2, 3))
    return (x + two) + (one + three)


def over_z(x):
    return x + lax.ppermute(x, "dp", [(d, d ^ 4) for d in range(64)])


def over_y(x):
    return sum_four(x, "dp", lambda k: [(d, d // 4 * 4 + (d + k) % 4) for d in range(64)])


def over_core(x):
    return x + lax.ppermute(x, "seq", [(s, s ^ 1) for s in range(8)])


def over_x(x):
    return sum_four(x, "seq", lambda k: [(s, (s + 2 * k) % 8) for s in range(8)])


def spread(pair):
    pad = jnp.zeros(pair.shape[:-2] + (16,), jnp.float32)
    return jnp.concatenate([pair[..., 0, :], pad, pair[..., 1, :], pad], axis=-1)


def windows(ids):
    first = ids[:, 0::BQ]
    last = ids[:, BQ - 1::BQ]
    lo = jnp.sum((ids[0][:, None] < first).astype(jnp.int32), axis=0)
    hi = jnp.sum((ids[0][:, None] <= last).astype(jnp.int32), axis=0)
    return (lo, hi)


def local(q_in, k_in, v_in, gain_q, gain_k, clip_ids):
    place = lax.axis_index("dp") % 8
    sent = shape((N_SEQ, BODY + EXTRA, HD))
    back = shape((N_SEQ, BODY + 2 * EXTRA, HD))
    inv = shape((TOK, HD), jnp.float32)
    here = pl.BlockSpec(memory_space=pltpu.VMEM)
    there = pl.BlockSpec(memory_space=pl.ANY)

    row = spread(jnp.stack([gain_q, gain_k]))[None]
    rows = jnp.where(lax.broadcasted_iota(jnp.int32, (8, HD), 0) == place, row, 0.0)
    rows = over_z(rows)

    pay, inv_q, inv_k, mark = pl.pallas_call(
        pack_kernel, out_shape=[sent, inv, inv, shape((8, HD), jnp.float32)],
        in_specs=[there] * 3, out_specs=[there, here, here, here],
        scratch_shapes=[pltpu.VMEM((2, TOK, WIDTH), jnp.bfloat16), pltpu.VMEM((EXTRA, HD), jnp.bfloat16),
                        pltpu.SemaphoreType.DMA((2 + 3 * H + N_SEQ,))],
        compiler_params=PARAMS, name="pack",
    )(q_in, k_in, v_in)
    got = lax.all_to_all(pay, "seq", 0, 0, tiled=True)
    rows = lax.ppermute(over_y(hold(rows, mark)), ("dp", "seq"), swapped())
    gain = jnp.stack([rows[:, 0:SHARD].reshape(-1), rows[:, 64:64 + SHARD].reshape(-1)])
    lo, hi = windows(clip_ids)

    half = pltpu.VMEM((HEADS, G, HD), jnp.bfloat16)
    full = pltpu.VMEM((G, HD), jnp.float32)
    turn = pltpu.VMEM((HEADS, HD, G), jnp.float32)
    few = pl.BlockSpec(memory_space=pltpu.SMEM)
    pay, dg = pl.pallas_call(
        attend_kernel, out_shape=[back, shape((2, HEADS * HD), jnp.float32)],
        in_specs=[few, few, here, here, here], out_specs=[there, here],
        scratch_shapes=[half] * 4 + [turn] * 2 + [full] * 2 + [
            pltpu.VMEM(back.shape, jnp.bfloat16), pltpu.SemaphoreType.DMA((N_SEQ,))],
        compiler_params=PARAMS, name="attend",
    )(lo, hi, got, gain, clip_ids)
    got = lax.all_to_all(pay, "seq", 0, 0, tiled=True)

    part = hold(spread(jnp.transpose(dg.reshape(2, N_SEQ, SHARD), (1, 0, 2))), dg)
    part = lax.ppermute(over_y(over_z(part)), ("dp", "seq"), swapped())
    part = over_x(over_core(part))
    part = lax.dynamic_index_in_dim(part, place, 0, keepdims=False)

    out = shape((TOK, WIDTH))
    d_q, d_k, d_v = pl.pallas_call(
        final_kernel, out_shape=[out] * 3, compiler_params=PARAMS, name="final",
    )(q_in, k_in, inv_q, inv_k, got)
    return (d_q, d_k, d_v, part[0:SHARD], part[64:64 + SHARD])


def solution(mesh):
    rows = P(("dp", "seq"), None)
    return jax.shard_map(
        local, mesh=mesh,
        in_specs=(rows, rows, rows, P("dp"), P("dp"), P("dp", None)),
        out_specs=(rows, rows, rows, P("dp"), P("dp")), check_vma=False)
```

```python
import jax
import jax.numpy as jnp
from jax import lax
from jax.experimental import pallas as pl
from jax.experimental.pallas import tpu as pltpu
from jax.sharding import PartitionSpec as P

H = 24
HD = 128
TOK = 128
N_SEQ = 8
HEADS = H // N_SEQ
G = TOK * N_SEQ
WIDTH = H * HD
BQ = 256
WINDOWS = (512, 640, 768, 1024)
EXTRA = 16
BODY = 3 * TOK * HEADS
EPS = 1e-06
SCALE = HD ** (-0.5)
LOG2E = 1.4426950408889634
SHARD = 48


def split3(x):
    hi = x.astype(jnp.bfloat16).astype(jnp.float32)
    mid = (x - hi).astype(jnp.bfloat16).astype(jnp.float32)
    return (hi, mid, x - hi - mid)


def extra_rows(rows, size):
    at = lax.broadcasted_iota(jnp.int32, (size, HD), 0)
    out = jnp.zeros((size, HD), jnp.float32)
    for index, piece in enumerate([piece for row in rows for piece in split3(row)]):
        out = jnp.where(at == index, piece, out)
    return out.astype(jnp.bfloat16)


def join3(extra, n):
    x = extra[3 * n:3 * n + 3]
    return (x[0:1] + x[1:2]) + x[2:3]


def column(row):
    return jnp.transpose(jnp.broadcast_to(row, (HD, HD)))


def body(c, n):
    return slice((c * 3 + n) * TOK, (c * 3 + n + 1) * TOK)


def pack_kernel(q_ref, k_ref, v_ref, pay_ref, inv_q_ref, inv_k_ref, mark_ref, held, extra, sems):
    loads = []
    for n, ref in enumerate((q_ref, k_ref)):
        loads.append(pltpu.make_async_copy(ref, held.at[n], sems.at[n]))
        loads[n].start()
    copies = []
    for s in range(N_SEQ):
        for c in range(HEADS):
            h = s * HEADS + c
            for n, ref in enumerate((q_ref, k_ref, v_ref)):
                copies.append(pltpu.make_async_copy(
                    ref.at[:, h * HD:(h + 1) * HD], pay_ref.at[s, body(c, n)], sems.at[2 + len(copies)]))
                copies[-1].start()
    rows = []
    for n, inv_ref in enumerate((inv_q_ref, inv_k_ref)):
        loads[n].wait()
        total = jnp.zeros((TOK, HD), jnp.float32)
        for h in range(H):
            x = held[n, :, h * HD:(h + 1) * HD].astype(jnp.float32)
            total = total + x * x
        inv = lax.rsqrt(jnp.sum(total, axis=1, keepdims=True) * (1.0 / WIDTH) + EPS)
        inv = jnp.broadcast_to(inv, (TOK, HD))
        inv_ref[...] = inv
        rows.append(jnp.transpose(inv)[0:1])
    mark_ref[...] = jnp.zeros_like(mark_ref)
    extra[...] = extra_rows(rows, EXTRA)
    for s in range(N_SEQ):
        copies.append(pltpu.make_async_copy(extra, pay_ref.at[s, BODY:], sems.at[2 + len(copies)]))
        copies[-1].start()
    for copy in copies:
        copy.wait()


def nt(a, b):
    return lax.dot_general(a, b, (((1,), (1,)), ((), ())), preferred_element_type=jnp.float32)


def nn(a, b):
    return jnp.dot(a, b, preferred_element_type=jnp.float32)


def gather_lanes(rows):
    lane = lax.broadcasted_iota(jnp.int32, (8, HD), 1)
    out = []
    for n in range(2):
        part = jnp.where(lane < SHARD, pltpu.roll(rows, (HD - 64 * n) % HD, 1), 0.0)
        part = jnp.concatenate([part, jnp.zeros((8, (HEADS - 1) * HD), jnp.float32)], axis=1)
        total = part[0:1]
        for j in range(1, 8):
            total = total + pltpu.roll(part, SHARD * j, 1)[j:j + 1]
        out.append(total)
    return out


def spread_lanes(wide):
    lane = lax.broadcasted_iota(jnp.int32, (8, HD), 1)
    at = lax.broadcasted_iota(jnp.int32, (8, HD), 0)
    out = jnp.zeros((8, HD), jnp.float32)
    for n in range(2):
        x = jnp.broadcast_to(wide[n], (8, HEADS * HD))
        for j in range(8):
            part = pltpu.roll(x, (HEADS * HD - SHARD * j) % (HEADS * HD), 1)[:, 0:HD]
            part = pltpu.roll(part, 64 * n, 1)
            keep = jnp.logical_and(at == j, jnp.logical_and(lane >= 64 * n, lane < 64 * n + SHARD))
            out = jnp.where(keep, part, out)
    return out


def attend_kernel(lo_ref, hi_ref, pay_ref, gain_ref, ids_ref, out_ref, dg_ref,
                  qn, kn, vv, dq, acc_k, acc_v, mq, mk, outs, sems):
    for j in range(N_SEQ):
        extra = pay_ref[j, BODY:].astype(jnp.float32)
        at = slice(j * TOK, (j + 1) * TOK)
        mq[at] = column(join3(extra, 0))
        mk[at] = column(join3(extra, 1))
    wide = gather_lanes(gain_ref[...])
    gains = [[wide[n][:, c * HD:(c + 1) * HD] for n in range(2)] for c in range(HEADS)]
    extra = extra_rows([row for pair in gains for row in pair], 2 * EXTRA)
    for j in range(N_SEQ):
        outs[j, BODY:] = extra

    def hats(c, j):
        at = slice(j * TOK, (j + 1) * TOK)
        return (pay_ref[j, body(c, 0)].astype(jnp.float32) * mq[at],
                pay_ref[j, body(c, 1)].astype(jnp.float32) * mk[at])

    for c in range(HEADS):
        for j in range(N_SEQ):
            q, k = hats(c, j)
            at = slice(j * TOK, (j + 1) * TOK)
            qn[c, at] = (q * gains[c][0]).astype(jnp.bfloat16)
            kn[c, at] = (k * gains[c][1]).astype(jnp.bfloat16)
            vv[c, at] = pay_ref[j, body(c, 2)]
    acc_k[...] = jnp.zeros_like(acc_k)
    acc_v[...] = jnp.zeros_like(acc_v)

    def block(b, first, width):
        first = pl.multiple_of(first, TOK)
        rows = pl.ds(pl.multiple_of(b * BQ, BQ), BQ)
        keys = pl.ds(first, width)
        own = [column(ids_ref[:, pl.ds(pl.multiple_of(b * BQ + t, HD), HD)])[:, 0:1] for t in range(0, BQ, HD)]
        same = jnp.concatenate(own, axis=0) == ids_ref[:, keys]
        qb = [qn[c, rows] for c in range(HEADS)]
        kb = [kn[c, keys] for c in range(HEADS)]
        vb = [vv[c, keys] for c in range(HEADS)]
        val = {}

        def score(c):
            val["s", c] = nt(qb[c], kb[c])

        def soft(c):
            s = jnp.where(same, val["s", c], -1e30)
            top = jnp.max(s, axis=1, keepdims=True)
            e = jnp.exp2((s - top) * (SCALE * LOG2E))
            val["p", c] = e * (1.0 / jnp.sum(e, axis=1, keepdims=True))
            val["pb", c] = val["p", c].astype(jnp.bfloat16)

        def mix(c):
            val["a", c] = nn(val["pb", c], vb[c]).astype(jnp.bfloat16)

        def back(c):
            val["dp", c] = nt(val["a", c], vb[c])

        def less(c):
            p, dp = val["p", c], val["dp", c]
            delta = jnp.sum(p * dp, axis=1, keepdims=True)
            val["ds", c] = (p * (dp - delta) * SCALE).astype(jnp.bfloat16)

        def values(c):
            acc_v[c, :, keys] += nn(jnp.transpose(val["a", c]), val["pb", c])

        def grads(c):
            dq[c, rows] = nn(val["ds", c], kb[c]).astype(jnp.bfloat16)
            acc_k[c, :, keys] += nn(jnp.transpose(qb[c]), val["ds", c])

        for stage in (score, soft, mix, back, less, values, grads):
            for c in range(HEADS):
                stage(c)

    def step(b, carry):
        low = lo_ref[b] // TOK * TOK
        span = hi_ref[b] - low
        done = None
        for width in WINDOWS:
            fits = span <= width
            now = fits if done is None else jnp.logical_and(fits, jnp.logical_not(done))
            done = fits

            @pl.when(now)
            def _():
                block(b, jnp.minimum(low, G - width), width)
        return carry

    lax.fori_loop(0, G // BQ, step, 0)

    copies = []
    for j in range(N_SEQ):
        at = slice(j * TOK, (j + 1) * TOK)
        for c in range(HEADS):
            outs[j, body(c, 0)] = dq[c, at]
            outs[j, body(c, 1)] = jnp.transpose(acc_k[c, :, at].astype(jnp.bfloat16))
            outs[j, body(c, 2)] = jnp.transpose(acc_v[c, :, at].astype(jnp.bfloat16))
        copies.append(pltpu.make_async_copy(outs.at[j], out_ref.at[j], sems.at[j]))
        copies[j].start()
    wide = [[], []]
    for c in range(HEADS):
        sums = [jnp.zeros((TOK, HD), jnp.float32)] * 2
        for j in range(N_SEQ):
            hat = hats(c, j)
            sums = [sums[n] + outs[j, body(c, n)].astype(jnp.float32) * hat[n] for n in range(2)]
        for n in range(2):
            wide[n].append(jnp.sum(sums[n], axis=0, keepdims=True))
    dg_ref[...] = spread_lanes([jnp.concatenate(rows, axis=1) for rows in wide])
    for copy in copies:
        copy.wait()


def final_kernel(q_ref, k_ref, inv_q_ref, inv_k_ref, pay_ref, dq_ref, dk_ref, dv_ref, held, outs, sems):
    pairs = [(s, c, slice((s * HEADS + c) * HD, (s * HEADS + c + 1) * HD))
             for s in range(N_SEQ) for c in range(HEADS)]
    loads = [pltpu.make_async_copy(ref, held.at[n], sems.at[n]) for n, ref in enumerate((q_ref, k_ref))]
    for load in loads:
        load.start()
    copies = []
    for s, c, cols in pairs:
        copies.append(pltpu.make_async_copy(
            pay_ref.at[s, body(c, 2)], dv_ref.at[:, cols], sems.at[2 + len(copies)]))
        copies[-1].start()
    extras = [pay_ref[s, BODY:].astype(jnp.float32) for s in range(N_SEQ)]
    for n, (inv_ref, out_ref) in enumerate(((inv_q_ref, dq_ref), (inv_k_ref, dk_ref))):
        loads[n].wait()
        inv = inv_ref[...]

        def parts(s, c, cols):
            dhat = pay_ref[s, body(c, n)].astype(jnp.float32) * join3(extras[s], 2 * c + n)
            return (dhat, held[n, :, cols].astype(jnp.float32) * inv)

        total = jnp.zeros((TOK, HD), jnp.float32)
        for pair in pairs:
            dhat, hat = parts(*pair)
            total = total + dhat * hat
        mean = jnp.sum(total, axis=1, keepdims=True) * (1.0 / WIDTH)
        for s in range(N_SEQ):
            for pair in pairs[s * HEADS:(s + 1) * HEADS]:
                dhat, hat = parts(*pair)
                outs[n, :, pair[2]] = (inv * (dhat - hat * mean)).astype(jnp.bfloat16)
            if s % 4 == 3:
                cols = slice((s - 3) * HEADS * HD, (s + 1) * HEADS * HD)
                copies.append(pltpu.make_async_copy(
                    outs.at[n, :, cols], out_ref.at[:, cols], sems.at[2 + len(copies)]))
                copies[-1].start()
    for copy in copies:
        copy.wait()


def hold_kernel(x_ref, after_ref, out_ref):
    out_ref[...] = x_ref[...]


def hold(x, after):
    return pl.pallas_call(
        hold_kernel, out_shape=shape(x.shape, jnp.float32),
        in_specs=[HERE, HERE], out_specs=HERE, name="hold", cost_estimate=pl.CostEstimate(flops=1 << 36, bytes_accessed=1 << 27, transcendentals=0),
    )(x, after)


def shape(dims, dtype=jnp.bfloat16):
    return jax.ShapeDtypeStruct(dims, dtype)


def params(mib):
    return pltpu.CompilerParams(vmem_limit_bytes=mib * 1024 * 1024)


HERE = pl.BlockSpec(memory_space=pltpu.VMEM)
THERE = pl.BlockSpec(memory_space=pltpu.HBM)
SCALARS = pl.BlockSpec(memory_space=pltpu.SMEM)


def swapped():
    return [((b * 8 + i) * 8 + s, (s * 8 + i) * 8 + b) for b in range(8) for i in range(8) for s in range(8)]


def sum_four(x, axis, pairs):
    one, two, three = (lax.ppermute(x, axis, pairs(k)) for k in (1, 2, 3))
    return (x + two) + (one + three)


def over_z(x):
    return x + lax.ppermute(x, "dp", [(d, d ^ 4) for d in range(64)])


def over_y(x):
    return sum_four(x, "dp", lambda k: [(d, d // 4 * 4 + (d + k) % 4) for d in range(64)])


def over_core(x):
    return x + lax.ppermute(x, "seq", [(s, s ^ 1) for s in range(8)])


def over_x(x):
    return sum_four(x, "seq", lambda k: [(s, (s + 2 * k) % 8) for s in range(8)])


def spread(pair):
    pad = jnp.zeros(pair.shape[:-2] + (16,), jnp.float32)
    return jnp.concatenate([pair[..., 0, :], pad, pair[..., 1, :], pad], axis=-1)


def attend_call(lo, hi, got, gain, ids):
    back = shape((N_SEQ, BODY + 2 * EXTRA, HD))
    half = pltpu.VMEM((HEADS, G, HD), jnp.bfloat16)
    full = pltpu.VMEM((G, HD), jnp.float32)
    turn = pltpu.VMEM((HEADS, HD, G), jnp.float32)
    return pl.pallas_call(
        attend_kernel, out_shape=[back, shape((8, HD), jnp.float32)],
        in_specs=[SCALARS, SCALARS, HERE, HERE, HERE], out_specs=[THERE, HERE],
        scratch_shapes=[half] * 4 + [turn] * 2 + [full] * 2 + [
            pltpu.VMEM(back.shape, jnp.bfloat16), pltpu.SemaphoreType.DMA((N_SEQ,))],
        compiler_params=params(60), name="attend",
    )(lo, hi, got, gain, ids)


def windows(ids):
    first = ids[:, 0::BQ]
    last = ids[:, BQ - 1::BQ]
    lo = jnp.sum((ids[0][:, None] < first).astype(jnp.int32), axis=0)
    hi = jnp.sum((ids[0][:, None] <= last).astype(jnp.int32), axis=0)
    return (lo, hi)


def local(q_in, k_in, v_in, gain_q, gain_k, clip_ids):
    place = lax.axis_index("dp") % 8
    inv = shape((TOK, HD), jnp.float32)
    pair = pltpu.VMEM((2, TOK, WIDTH), jnp.bfloat16)

    row = spread(jnp.stack([gain_q, gain_k]))[None]
    rows = jnp.where(lax.broadcasted_iota(jnp.int32, (8, HD), 0) == place, row, 0.0)
    rows = over_z(rows)

    pay, inv_q, inv_k, mark = pl.pallas_call(
        pack_kernel,
        out_shape=[shape((N_SEQ, BODY + EXTRA, HD)), inv, inv, shape((8, HD), jnp.float32)],
        in_specs=[THERE] * 3, out_specs=[THERE, HERE, HERE, HERE],
        scratch_shapes=[pair, pltpu.VMEM((EXTRA, HD), jnp.bfloat16),
                        pltpu.SemaphoreType.DMA((2 + 3 * H + N_SEQ,))],
        compiler_params=params(62), name="pack",
    )(q_in, k_in, v_in)
    got = lax.all_to_all(pay, "seq", 0, 0, tiled=True)
    rows = lax.ppermute(over_y(hold(rows, mark)), ("dp", "seq"), swapped())
    lo, hi = windows(clip_ids)
    pay, part = attend_call(lo, hi, got, rows, clip_ids)

    blocks = [list(range(b, b + 8)) for b in range(0, 64, 8)]
    part = lax.all_to_all(part, "dp", 0, 0, axis_index_groups=blocks, tiled=True)
    part = jnp.sum(part, axis=0, keepdims=True)
    pay, part = lax.optimization_barrier((pay, part))
    got = lax.all_to_all(pay, "seq", 0, 0, tiled=True)
    part = hold(part, part)
    part = over_x(over_core(lax.ppermute(part, ("dp", "seq"), swapped())))[0]

    out = shape((TOK, WIDTH))
    d_q, d_k, d_v = pl.pallas_call(
        final_kernel, out_shape=[out] * 3,
        in_specs=[THERE, THERE, HERE, HERE, HERE], out_specs=[THERE] * 3,
        scratch_shapes=[pair, pair, pltpu.SemaphoreType.DMA((2 + H + 4,))],
        compiler_params=params(61), name="final",
    )(q_in, k_in, inv_q, inv_k, got)
    return (d_q, d_k, d_v, part[0:SHARD], part[64:64 + SHARD])


def solution(mesh):
    rows = P(("dp", "seq"), None)
    return jax.shard_map(
        local, mesh=mesh,
        in_specs=(rows, rows, rows, P("dp"), P("dp"), P("dp", None)),
        out_specs=(rows, rows, rows, P("dp"), P("dp")), check_vma=False)
```

```python
import jax
import jax.numpy as jnp
from jax import lax
from jax.experimental import pallas as pl
from jax.experimental.pallas import tpu as pltpu
from jax.sharding import PartitionSpec as P

H = 24
HD = 128
TOK = 128
N_SEQ = 8
HEADS = H // N_SEQ
G = TOK * N_SEQ
WIDTH = H * HD
BQ = 256
WINDOWS = (512, 640, 768, 1024)
EXTRA = 16
BODY = 3 * TOK * HEADS
EPS = 1e-06
SCALE = HD ** (-0.5)
LOG2E = 1.4426950408889634
SHARD = 48


def split3(x):
    hi = x.astype(jnp.bfloat16).astype(jnp.float32)
    mid = (x - hi).astype(jnp.bfloat16).astype(jnp.float32)
    return (hi, mid, x - hi - mid)


def extra_rows(rows, size):
    at = lax.broadcasted_iota(jnp.int32, (size, HD), 0)
    out = jnp.zeros((size, HD), jnp.float32)
    for index, piece in enumerate([piece for row in rows for piece in split3(row)]):
        out = jnp.where(at == index, piece, out)
    return out.astype(jnp.bfloat16)


def join3(extra, n):
    x = extra[3 * n:3 * n + 3]
    return (x[0:1] + x[1:2]) + x[2:3]


def column(row):
    return jnp.transpose(jnp.broadcast_to(row, (HD, HD)))


def body(c, n):
    return slice((c * 3 + n) * TOK, (c * 3 + n + 1) * TOK)


def pack_kernel(turn_ref, q_ref, k_ref, v_ref, pay_ref, inv_q_ref, inv_k_ref, mark_ref, held, extra, sems):
    loads = []
    for n, ref in enumerate((q_ref, k_ref, v_ref)):
        loads.append(pltpu.make_async_copy(ref, held.at[n], sems.at[n]))
        loads[n].start()
    dest = [(g + N_SEQ - turn_ref[0]) % N_SEQ for g in range(N_SEQ)]
    copies = []
    for n in range(3):
        loads[n].wait()
        for g in range(N_SEQ):
            for c in range(HEADS):
                h = g * HEADS + c
                copies.append(pltpu.make_async_copy(
                    held.at[n, :, h * HD:(h + 1) * HD], pay_ref.at[dest[g], body(c, n)], sems.at[3 + len(copies)]))
                copies[-1].start()
    rows = []
    for n, inv_ref in enumerate((inv_q_ref, inv_k_ref)):
        total = jnp.zeros((TOK, HD), jnp.float32)
        for h in range(H):
            x = held[n, :, h * HD:(h + 1) * HD].astype(jnp.float32)
            total = total + x * x
        inv = lax.rsqrt(jnp.sum(total, axis=1, keepdims=True) * (1.0 / WIDTH) + EPS)
        inv = jnp.broadcast_to(inv, (TOK, HD))
        inv_ref[...] = inv
        rows.append(jnp.transpose(inv)[0:1])
    mark_ref[...] = jnp.zeros_like(mark_ref)
    extra[...] = extra_rows(rows, EXTRA)
    for s in range(N_SEQ):
        copies.append(pltpu.make_async_copy(extra, pay_ref.at[s, BODY:], sems.at[3 + len(copies)]))
        copies[-1].start()
    for copy in copies:
        copy.wait()


def nt(a, b):
    return lax.dot_general(a, b, (((1,), (1,)), ((), ())), preferred_element_type=jnp.float32)


def nn(a, b):
    return jnp.dot(a, b, preferred_element_type=jnp.float32)


def gather_lanes(rows):
    lane = lax.broadcasted_iota(jnp.int32, (8, HD), 1)
    out = []
    for n in range(2):
        part = jnp.where(lane < SHARD, pltpu.roll(rows, (HD - 64 * n) % HD, 1), 0.0)
        part = jnp.concatenate([part, jnp.zeros((8, (HEADS - 1) * HD), jnp.float32)], axis=1)
        total = part[0:1]
        for j in range(1, 8):
            total = total + pltpu.roll(part, SHARD * j, 1)[j:j + 1]
        out.append(total)
    return out


def spread_lanes(wide):
    lane = lax.broadcasted_iota(jnp.int32, (8, HD), 1)
    at = lax.broadcasted_iota(jnp.int32, (8, HD), 0)
    out = jnp.zeros((8, HD), jnp.float32)
    for n in range(2):
        x = jnp.broadcast_to(wide[n], (8, HEADS * HD))
        for j in range(8):
            part = pltpu.roll(x, (HEADS * HD - SHARD * j) % (HEADS * HD), 1)[:, 0:HD]
            part = pltpu.roll(part, 64 * n, 1)
            keep = jnp.logical_and(at == j, jnp.logical_and(lane >= 64 * n, lane < 64 * n + SHARD))
            out = jnp.where(keep, part, out)
    return out


def attend_kernel(lo_ref, hi_ref, pay_ref, gain_ref, ids_ref, out_ref, dg_ref,
                  qn, kn, vv, dq, acc_k, acc_v, mq, mk, outs, sems):
    for j in range(N_SEQ):
        extra = pay_ref[j, BODY:].astype(jnp.float32)
        at = slice(j * TOK, (j + 1) * TOK)
        mq[at] = column(join3(extra, 0))
        mk[at] = column(join3(extra, 1))
    wide = gather_lanes(gain_ref[...])
    gains = [[wide[n][:, c * HD:(c + 1) * HD] for n in range(2)] for c in range(HEADS)]
    extra = extra_rows([row for pair in gains for row in pair], 2 * EXTRA)
    for j in range(N_SEQ):
        outs[j, BODY:] = extra

    def hats(c, j):
        at = slice(j * TOK, (j + 1) * TOK)
        return (pay_ref[j, body(c, 0)].astype(jnp.float32) * mq[at],
                pay_ref[j, body(c, 1)].astype(jnp.float32) * mk[at])

    for c in range(HEADS):
        for j in range(N_SEQ):
            q, k = hats(c, j)
            at = slice(j * TOK, (j + 1) * TOK)
            qn[c, at] = (q * gains[c][0]).astype(jnp.bfloat16)
            kn[c, at] = (k * gains[c][1]).astype(jnp.bfloat16)
            vv[c, at] = pay_ref[j, body(c, 2)]
    acc_k[...] = jnp.zeros_like(acc_k)
    acc_v[...] = jnp.zeros_like(acc_v)

    def block(b, first, width):
        first = pl.multiple_of(first, TOK)
        rows = pl.ds(pl.multiple_of(b * BQ, BQ), BQ)
        keys = pl.ds(first, width)
        own = [column(ids_ref[:, pl.ds(pl.multiple_of(b * BQ + t, HD), HD)])[:, 0:1] for t in range(0, BQ, HD)]
        same = jnp.concatenate(own, axis=0) == ids_ref[:, keys]
        qb = [qn[c, rows] for c in range(HEADS)]
        kb = [kn[c, keys] for c in range(HEADS)]
        vb = [vv[c, keys] for c in range(HEADS)]
        val = {}

        def score(c):
            val["s", c] = nt(qb[c], kb[c])

        def soft(c):
            s = jnp.where(same, val["s", c], -1e30)
            top = jnp.max(s, axis=1, keepdims=True)
            e = jnp.exp2((s - top) * (SCALE * LOG2E))
            val["p", c] = e * (1.0 / jnp.sum(e, axis=1, keepdims=True))
            val["pb", c] = val["p", c].astype(jnp.bfloat16)

        def mix(c):
            val["a", c] = nn(val["pb", c], vb[c]).astype(jnp.bfloat16)

        def back(c):
            val["dp", c] = nt(val["a", c], vb[c])

        def less(c):
            p, dp = val["p", c], val["dp", c]
            delta = jnp.sum(p * dp, axis=1, keepdims=True)
            val["ds", c] = (p * (dp - delta) * SCALE).astype(jnp.bfloat16)

        def values(c):
            acc_v[c, :, keys] += nn(jnp.transpose(val["a", c]), val["pb", c])

        def grads(c):
            dq[c, rows] = nn(val["ds", c], kb[c]).astype(jnp.bfloat16)
            acc_k[c, :, keys] += nn(jnp.transpose(qb[c]), val["ds", c])

        for stage in (score, soft, mix, back, less, values, grads):
            for c in range(HEADS):
                stage(c)

    def step(b, carry):
        low = lo_ref[b] // TOK * TOK
        span = hi_ref[b] - low
        done = None
        for width in WINDOWS:
            fits = span <= width
            now = fits if done is None else jnp.logical_and(fits, jnp.logical_not(done))
            done = fits

            @pl.when(now)
            def _():
                block(b, jnp.minimum(low, G - width), width)
        return carry

    lax.fori_loop(0, G // BQ, step, 0)

    copies = []
    for j in range(N_SEQ):
        at = slice(j * TOK, (j + 1) * TOK)
        for c in range(HEADS):
            outs[j, body(c, 0)] = dq[c, at]
            outs[j, body(c, 1)] = jnp.transpose(acc_k[c, :, at].astype(jnp.bfloat16))
            outs[j, body(c, 2)] = jnp.transpose(acc_v[c, :, at].astype(jnp.bfloat16))
        copies.append(pltpu.make_async_copy(outs.at[j], out_ref.at[j], sems.at[j]))
        copies[j].start()
    wide = [[], []]
    for c in range(HEADS):
        sums = [jnp.zeros((TOK, HD), jnp.float32)] * 2
        for j in range(N_SEQ):
            hat = hats(c, j)
            sums = [sums[n] + outs[j, body(c, n)].astype(jnp.float32) * hat[n] for n in range(2)]
        for n in range(2):
            wide[n].append(jnp.sum(sums[n], axis=0, keepdims=True))
    dg_ref[...] = spread_lanes([jnp.concatenate(rows, axis=1) for rows in wide])
    for copy in copies:
        copy.wait()


def final_kernel(turn_ref, q_ref, k_ref, inv_q_ref, inv_k_ref, pay_ref, dq_ref, dk_ref, dv_ref, outs, sems):
    src = [(g + N_SEQ - turn_ref[0]) % N_SEQ for g in range(N_SEQ)]
    pairs = [(g, c, slice((g * HEADS + c) * HD, (g * HEADS + c + 1) * HD))
             for g in range(N_SEQ) for c in range(HEADS)]
    copies = []

    def send(n, ref):
        copies.append(pltpu.make_async_copy(outs.at[n], ref, sems.at[n]))
        copies[-1].start()

    for g, c, cols in pairs:
        outs[2, :, cols] = pay_ref[src[g], body(c, 2)]
    send(2, dv_ref)
    extras = [pay_ref[src[g], BODY:].astype(jnp.float32) for g in range(N_SEQ)]
    for n, (ref, inv_ref, out_ref) in enumerate(((q_ref, inv_q_ref, dq_ref), (k_ref, inv_k_ref, dk_ref))):
        inv = inv_ref[...]

        def parts(g, c, cols):
            dhat = pay_ref[src[g], body(c, n)].astype(jnp.float32) * join3(extras[g], 2 * c + n)
            return (dhat, ref[:, cols].astype(jnp.float32) * inv)

        total = jnp.zeros((TOK, HD), jnp.float32)
        for pair in pairs:
            dhat, hat = parts(*pair)
            total = total + dhat * hat
        mean = jnp.sum(total, axis=1, keepdims=True) * (1.0 / WIDTH)
        for pair in pairs:
            dhat, hat = parts(*pair)
            outs[n, :, pair[2]] = (inv * (dhat - hat * mean)).astype(jnp.bfloat16)
        send(n, out_ref)
    for copy in copies:
        copy.wait()


def hold_kernel(x_ref, after_ref, out_ref):
    out_ref[...] = x_ref[...]


def hold(x, after):
    return pl.pallas_call(
        hold_kernel, out_shape=shape(x.shape, jnp.float32),
        in_specs=[HERE, HERE], out_specs=HERE,
        compiler_params=params(1), name="hold", cost_estimate=pl.CostEstimate(flops=1 << 36, bytes_accessed=1 << 27, transcendentals=0),
    )(x, after)


def shape(dims, dtype=jnp.bfloat16):
    return jax.ShapeDtypeStruct(dims, dtype)


def params(mib):
    return pltpu.CompilerParams(vmem_limit_bytes=mib * 1024 * 1024)


HERE = pl.BlockSpec(memory_space=pltpu.VMEM)
THERE = pl.BlockSpec(memory_space=pltpu.HBM)
SCALARS = pl.BlockSpec(memory_space=pltpu.SMEM)


def around(way):
    return [((b * 8 + i) * 8 + s, ((b + way * s) % 8 * 8 + i) * 8 + s)
            for b in range(8) for i in range(8) for s in range(8)]


def sum_four(x, axis, pairs):
    one, two, three = (lax.ppermute(x, axis, pairs(k)) for k in (1, 2, 3))
    return (x + two) + (one + three)


def over_z(x):
    return x + lax.ppermute(x, "dp", [(d, d ^ 4) for d in range(64)])


def over_y(x):
    return sum_four(x, "dp", lambda k: [(d, d // 4 * 4 + (d + k) % 4) for d in range(64)])


def over_core(x):
    return x + lax.ppermute(x, "seq", [(s, s ^ 1) for s in range(8)])


def over_x(x):
    return sum_four(x, "seq", lambda k: [(s, (s + 2 * k) % 8) for s in range(8)])


def spread(pair):
    pad = jnp.zeros(pair.shape[:-2] + (16,), jnp.float32)
    return jnp.concatenate([pair[..., 0, :], pad, pair[..., 1, :], pad], axis=-1)


def attend_call(lo, hi, got, gain, ids):
    back = shape((N_SEQ, BODY + 2 * EXTRA, HD))
    half = pltpu.VMEM((HEADS, G, HD), jnp.bfloat16)
    full = pltpu.VMEM((G, HD), jnp.float32)
    turn = pltpu.VMEM((HEADS, HD, G), jnp.float32)
    return pl.pallas_call(
        attend_kernel, out_shape=[back, shape((8, HD), jnp.float32)],
        in_specs=[SCALARS, SCALARS, HERE, HERE, HERE], out_specs=[THERE, HERE],
        scratch_shapes=[half] * 4 + [turn] * 2 + [full] * 2 + [
            pltpu.VMEM(back.shape, jnp.bfloat16), pltpu.SemaphoreType.DMA((N_SEQ,))],
        compiler_params=params(44), name="attend",
    )(lo, hi, got, gain, ids)


def windows(ids):
    first = ids[:, 0::BQ]
    last = ids[:, BQ - 1::BQ]
    lo = jnp.sum((ids[0][:, None] < first).astype(jnp.int32), axis=0)
    hi = jnp.sum((ids[0][:, None] <= last).astype(jnp.int32), axis=0)
    return (lo, hi)


def local(q_in, k_in, v_in, gain_q, gain_k, clip_ids):
    place = lax.axis_index("dp") % 8
    turn = (lax.axis_index("dp") // 8).astype(jnp.int32)[None]
    inv = shape((TOK, HD), jnp.float32)
    three = pltpu.VMEM((3, TOK, WIDTH), jnp.bfloat16)

    row = spread(jnp.stack([gain_q, gain_k]))[None]
    rows = jnp.where(lax.broadcasted_iota(jnp.int32, (8, HD), 0) == place, row, 0.0)

    pay, inv_q, inv_k, mark = pl.pallas_call(
        pack_kernel,
        out_shape=[shape((N_SEQ, BODY + EXTRA, HD)), inv, inv, shape((8, HD), jnp.float32)],
        in_specs=[SCALARS] + [THERE] * 3, out_specs=[THERE, HERE, HERE, HERE],
        scratch_shapes=[three, pltpu.VMEM((EXTRA, HD), jnp.bfloat16),
                        pltpu.SemaphoreType.DMA((3 + 3 * H + N_SEQ,))],
        compiler_params=params(62), name="pack",
    )(turn, q_in, k_in, v_in)
    got = lax.all_to_all(pay, "seq", 0, 0, tiled=True)
    rows = lax.ppermute(over_y(over_z(hold(rows, mark))), ("dp", "seq"), around(-1))
    lo, hi = windows(clip_ids)
    pay, part = attend_call(lo, hi, got, rows, clip_ids)

    blocks = [list(range(b, b + 8)) for b in range(0, 64, 8)]
    part = lax.all_to_all(part, "dp", 0, 0, axis_index_groups=blocks, tiled=True)
    part = jnp.sum(part, axis=0, keepdims=True)
    pay, part = lax.optimization_barrier((pay, part))
    got = lax.all_to_all(pay, "seq", 0, 0, tiled=True)
    part = hold(part, part)
    part = over_x(over_core(lax.ppermute(part, ("dp", "seq"), around(1))))[0]

    out = shape((TOK, WIDTH))
    d_q, d_k, d_v = pl.pallas_call(
        final_kernel, out_shape=[out] * 3,
        in_specs=[SCALARS] + [HERE] * 5, out_specs=[THERE] * 3,
        scratch_shapes=[three, pltpu.SemaphoreType.DMA((3,))],
        compiler_params=params(16), name="final",
        cost_estimate=pl.CostEstimate(flops=1 << 34, bytes_accessed=1 << 25, transcendentals=0),
    )(turn, q_in, k_in, inv_q, inv_k, got)
    return (d_q, d_k, d_v, part[0:SHARD], part[64:64 + SHARD])


def solution(mesh):
    rows = P(("dp", "seq"), None)
    return jax.shard_map(
        local, mesh=mesh,
        in_specs=(rows, rows, rows, P("dp"), P("dp"), P("dp", None)),
        out_specs=(rows, rows, rows, P("dp"), P("dp")), check_vma=False)
```

```python
import jax
import jax.numpy as jnp
from jax import lax
from jax.experimental import pallas as pl
from jax.experimental.pallas import tpu as pltpu
from jax.sharding import PartitionSpec as P

H = 24
HD = 128
TOK = 128
N_SEQ = 8
HEADS = H // N_SEQ
G = TOK * N_SEQ
WIDTH = H * HD
BQ = 256
PAIR = 1
WINDOWS = (384, 512, 640, 768, 896, 1024)
EXTRA = 16
BODY = 3 * TOK * HEADS
EPS = 1e-06
SCALE = HD ** (-0.5)
LOG2E = 1.4426950408889634
SHARD = 48
CUTS = 4


def split3(x):
    hi = x.astype(jnp.bfloat16).astype(jnp.float32)
    mid = (x - hi).astype(jnp.bfloat16).astype(jnp.float32)
    return (hi, mid, x - hi - mid)


def extra_rows(rows, size):
    at = lax.broadcasted_iota(jnp.int32, (size, HD), 0)
    out = jnp.zeros((size, HD), jnp.float32)
    for index, piece in enumerate([piece for row in rows for piece in split3(row)]):
        out = jnp.where(at == index, piece, out)
    return out.astype(jnp.bfloat16)


def join3(extra, n):
    x = extra[3 * n:3 * n + 3]
    return (x[0:1] + x[1:2]) + x[2:3]


def column(row):
    return jnp.transpose(jnp.broadcast_to(row, (HD, HD)))


def body(c, n):
    return slice((c * 3 + n) * TOK, (c * 3 + n + 1) * TOK)


def pack_kernel(turn_ref, q_ref, k_ref, v_ref, pay_ref, inv_q_ref, inv_k_ref, mark_ref, held, extra, load_sems, sems):
    wide = WIDTH // CUTS
    loads = []
    for t in range(CUTS):
        cols = slice(t * wide, (t + 1) * wide)
        for n, ref in enumerate((q_ref, k_ref, v_ref)):
            loads.append(pltpu.make_async_copy(ref.at[:, cols], held.at[n, :, cols], load_sems.at[len(loads)]))
            loads[-1].start()
    copies = []
    for t in range(CUTS):
        for n in range(3):
            loads[3 * t + n].wait()
            for h in range(t * H // CUTS, (t + 1) * H // CUTS):
                dest = (h // HEADS + N_SEQ - turn_ref[0]) % N_SEQ
                copies.append(pltpu.make_async_copy(
                    held.at[n, :, h * HD:(h + 1) * HD], pay_ref.at[dest, body(h % HEADS, n)], sems.at[len(copies)]))
                copies[-1].start()
    rows = []
    for n, inv_ref in enumerate((inv_q_ref, inv_k_ref)):
        total = jnp.zeros((TOK, HD), jnp.float32)
        for h in range(H):
            x = held[n, :, h * HD:(h + 1) * HD].astype(jnp.float32)
            total = total + x * x
        inv = lax.rsqrt(jnp.sum(total, axis=1, keepdims=True) * (1.0 / WIDTH) + EPS)
        inv = jnp.broadcast_to(inv, (TOK, HD))
        inv_ref[...] = inv
        rows.append(jnp.transpose(inv)[0:1])
    mark_ref[...] = jnp.zeros_like(mark_ref)
    extra[...] = extra_rows(rows, EXTRA)
    for s in range(N_SEQ):
        copies.append(pltpu.make_async_copy(extra, pay_ref.at[s, BODY:], sems.at[len(copies)]))
        copies[-1].start()
    for copy in copies:
        copy.wait()


def nt(a, b):
    return lax.dot_general(a, b, (((1,), (1,)), ((), ())), preferred_element_type=jnp.float32)


def nn(a, b):
    return jnp.dot(a, b, preferred_element_type=jnp.float32)


def gather_lanes(rows):
    lane = lax.broadcasted_iota(jnp.int32, (8, HD), 1)
    out = []
    for n in range(2):
        part = jnp.where(lane < SHARD, pltpu.roll(rows, (HD - 64 * n) % HD, 1), 0.0)
        part = jnp.concatenate([part, jnp.zeros((8, (HEADS - 1) * HD), jnp.float32)], axis=1)
        total = part[0:1]
        for j in range(1, 8):
            total = total + pltpu.roll(part, SHARD * j, 1)[j:j + 1]
        out.append(total)
    return out


def spread_lanes(wide):
    lane = lax.broadcasted_iota(jnp.int32, (8, HD), 1)
    at = lax.broadcasted_iota(jnp.int32, (8, HD), 0)
    out = jnp.zeros((8, HD), jnp.float32)
    for n in range(2):
        x = jnp.broadcast_to(wide[n], (8, HEADS * HD))
        for j in range(8):
            part = pltpu.roll(x, (HEADS * HD - SHARD * j) % (HEADS * HD), 1)[:, 0:HD]
            part = pltpu.roll(part, 64 * n, 1)
            keep = jnp.logical_and(at == j, jnp.logical_and(lane >= 64 * n, lane < 64 * n + SHARD))
            out = jnp.where(keep, part, out)
    return out


def attend_kernel(lo_ref, hi_ref, pay_ref, gain_ref, ids_ref, out_ref, dg_ref,
                  qn, kn, vv, dq, acc_k, acc_v, mq, mk, outs, sems):
    for j in range(N_SEQ):
        extra = pay_ref[j, BODY:].astype(jnp.float32)
        at = slice(j * TOK, (j + 1) * TOK)
        mq[at] = column(join3(extra, 0))
        mk[at] = column(join3(extra, 1))
    wide = gather_lanes(gain_ref[...])
    gains = [[wide[n][:, c * HD:(c + 1) * HD] for n in range(2)] for c in range(HEADS)]
    extra = extra_rows([row for pair in gains for row in pair], 2 * EXTRA)
    for j in range(N_SEQ):
        outs[j, BODY:] = extra

    def hats(c, j):
        at = slice(j * TOK, (j + 1) * TOK)
        return (pay_ref[j, body(c, 0)].astype(jnp.float32) * mq[at],
                pay_ref[j, body(c, 1)].astype(jnp.float32) * mk[at])

    for c in range(HEADS):
        for j in range(N_SEQ):
            q, k = hats(c, j)
            at = slice(j * TOK, (j + 1) * TOK)
            qn[c, at] = (q * gains[c][0]).astype(jnp.bfloat16)
            kn[c, at] = (k * gains[c][1]).astype(jnp.bfloat16)
            vv[c, at] = pay_ref[j, body(c, 2)]
    acc_k[...] = jnp.zeros_like(acc_k)
    acc_v[...] = jnp.zeros_like(acc_v)

    def blocks(b, first, width):
        units = [(t, c) for t in range(PAIR) for c in range(HEADS)]
        start = [pl.multiple_of(f, TOK) for f in first]
        rows = [pl.ds(pl.multiple_of((b * PAIR + t) * BQ, BQ), BQ) for t in range(PAIR)]
        keys = [pl.ds(f, width) for f in start]
        same = []
        for t in range(PAIR):
            own = [column(ids_ref[:, pl.ds(pl.multiple_of((b * PAIR + t) * BQ + r, HD), HD)])[:, 0:1]
                   for r in range(0, BQ, HD)]
            same.append(jnp.concatenate(own, axis=0) == ids_ref[:, keys[t]])
        qb = {(t, c): qn[c, rows[t]] for t, c in units}
        kb = {(t, c): kn[c, keys[t]] for t, c in units}
        vb = {(t, c): vv[c, keys[t]] for t, c in units}
        val = {}

        def score(u):
            val["s", u] = nt(qb[u], kb[u])

        def soft(u):
            s = jnp.where(same[u[0]], val["s", u], -1e30)
            top = jnp.max(s, axis=1, keepdims=True)
            e = jnp.exp2((s - top) * (SCALE * LOG2E))
            val["p", u] = e * (1.0 / jnp.sum(e, axis=1, keepdims=True))
            val["pb", u] = val["p", u].astype(jnp.bfloat16)

        def mix(u):
            val["a", u] = nn(val["pb", u], vb[u]).astype(jnp.bfloat16)

        def back(u):
            val["dp", u] = nt(val["a", u], vb[u])

        def less(u):
            p, dp = val["p", u], val["dp", u]
            delta = jnp.sum(p * dp, axis=1, keepdims=True)
            val["ds", u] = (p * (dp - delta) * SCALE).astype(jnp.bfloat16)

        def values(u):
            acc_v[u[1], :, keys[u[0]]] += nn(jnp.transpose(val["a", u]), val["pb", u])

        def grads(u):
            dq[u[1], rows[u[0]]] = nn(val["ds", u], kb[u]).astype(jnp.bfloat16)
            acc_k[u[1], :, keys[u[0]]] += nn(jnp.transpose(qb[u]), val["ds", u])

        for stage in (score, soft, mix, back, less, values, grads):
            for u in units:
                stage(u)

    def step(b, carry):
        low = [lo_ref[b * PAIR + t] // TOK * TOK for t in range(PAIR)]
        span = hi_ref[b * PAIR] - low[0]
        for t in range(1, PAIR):
            span = jnp.maximum(span, hi_ref[b * PAIR + t] - low[t])
        done = None
        for width in WINDOWS:
            fits = span <= width
            now = fits if done is None else jnp.logical_and(fits, jnp.logical_not(done))
            done = fits

            @pl.when(now)
            def _():
                blocks(b, [jnp.minimum(f, G - width) for f in low], width)
        return carry

    lax.fori_loop(0, G // BQ // PAIR, step, 0)

    copies = []
    for j in range(N_SEQ):
        at = slice(j * TOK, (j + 1) * TOK)
        for c in range(HEADS):
            outs[j, body(c, 0)] = dq[c, at]
            outs[j, body(c, 1)] = jnp.transpose(acc_k[c, :, at].astype(jnp.bfloat16))
            outs[j, body(c, 2)] = jnp.transpose(acc_v[c, :, at].astype(jnp.bfloat16))
        copies.append(pltpu.make_async_copy(outs.at[j], out_ref.at[j], sems.at[j]))
        copies[j].start()
    wide = [[], []]
    for c in range(HEADS):
        sums = [jnp.zeros((TOK, HD), jnp.float32)] * 2
        for j in range(N_SEQ):
            hat = hats(c, j)
            sums = [sums[n] + outs[j, body(c, n)].astype(jnp.float32) * hat[n] for n in range(2)]
        for n in range(2):
            wide[n].append(jnp.sum(sums[n], axis=0, keepdims=True))
    dg_ref[...] = spread_lanes([jnp.concatenate(rows, axis=1) for rows in wide])
    for copy in copies:
        copy.wait()


def final_kernel(turn_ref, q_ref, k_ref, inv_q_ref, inv_k_ref, pay_ref, dq_ref, dk_ref, dv_ref, outs, sems):
    src = [(g + N_SEQ - turn_ref[0]) % N_SEQ for g in range(N_SEQ)]
    pairs = [(g, c, slice((g * HEADS + c) * HD, (g * HEADS + c + 1) * HD))
             for g in range(N_SEQ) for c in range(HEADS)]
    copies = []

    def send(n, ref):
        copies.append(pltpu.make_async_copy(outs.at[n], ref, sems.at[n]))
        copies[-1].start()

    for g, c, cols in pairs:
        outs[2, :, cols] = pay_ref[src[g], body(c, 2)]
    send(2, dv_ref)
    extras = [pay_ref[src[g], BODY:].astype(jnp.float32) for g in range(N_SEQ)]
    for n, (ref, inv_ref, out_ref) in enumerate(((q_ref, inv_q_ref, dq_ref), (k_ref, inv_k_ref, dk_ref))):
        inv = inv_ref[...]

        def parts(g, c, cols):
            dhat = pay_ref[src[g], body(c, n)].astype(jnp.float32) * join3(extras[g], 2 * c + n)
            return (dhat, ref[:, cols].astype(jnp.float32) * inv)

        total = jnp.zeros((TOK, HD), jnp.float32)
        for pair in pairs:
            dhat, hat = parts(*pair)
            total = total + dhat * hat
        mean = jnp.sum(total, axis=1, keepdims=True) * (1.0 / WIDTH)
        for pair in pairs:
            dhat, hat = parts(*pair)
            outs[n, :, pair[2]] = (inv * (dhat - hat * mean)).astype(jnp.bfloat16)
        send(n, out_ref)
    for copy in copies:
        copy.wait()


def hold_kernel(x_ref, after_ref, out_ref):
    out_ref[...] = x_ref[...]


def hold(x, after):
    return pl.pallas_call(
        hold_kernel, out_shape=shape(x.shape, jnp.float32),
        in_specs=[HERE, HERE], out_specs=HERE,
        compiler_params=params(1), name="hold", cost_estimate=pl.CostEstimate(flops=1 << 36, bytes_accessed=1 << 27, transcendentals=0),
    )(x, after)


def shape(dims, dtype=jnp.bfloat16):
    return jax.ShapeDtypeStruct(dims, dtype)


def params(mib):
    return pltpu.CompilerParams(vmem_limit_bytes=mib * 1024 * 1024)


HERE = pl.BlockSpec(memory_space=pltpu.VMEM)
THERE = pl.BlockSpec(memory_space=pltpu.HBM)
SCALARS = pl.BlockSpec(memory_space=pltpu.SMEM)


def around(way):
    return [((b * 8 + i) * 8 + s, ((b + way * s) % 8 * 8 + i) * 8 + s)
            for b in range(8) for i in range(8) for s in range(8)]


def sum_four(x, axis, pairs):
    one, two, three = (lax.ppermute(x, axis, pairs(k)) for k in (1, 2, 3))
    return (x + two) + (one + three)


def over_z(x):
    return x + lax.ppermute(x, "dp", [(d, d ^ 4) for d in range(64)])


def over_y(x):
    return sum_four(x, "dp", lambda k: [(d, d // 4 * 4 + (d + k) % 4) for d in range(64)])


def over_core(x):
    return x + lax.ppermute(x, "seq", [(s, s ^ 1) for s in range(8)])


def over_x(x):
    return sum_four(x, "seq", lambda k: [(s, (s + 2 * k) % 8) for s in range(8)])


def spread(pair):
    pad = jnp.zeros(pair.shape[:-2] + (16,), jnp.float32)
    return jnp.concatenate([pair[..., 0, :], pad, pair[..., 1, :], pad], axis=-1)


def attend_call(lo, hi, got, gain, ids):
    back = shape((N_SEQ, BODY + 2 * EXTRA, HD))
    half = pltpu.VMEM((HEADS, G, HD), jnp.bfloat16)
    full = pltpu.VMEM((G, HD), jnp.float32)
    turn = pltpu.VMEM((HEADS, HD, G), jnp.float32)
    return pl.pallas_call(
        attend_kernel, out_shape=[back, shape((8, HD), jnp.float32)],
        in_specs=[SCALARS, SCALARS, HERE, HERE, HERE], out_specs=[THERE, HERE],
        scratch_shapes=[half] * 4 + [turn] * 2 + [full] * 2 + [
            pltpu.VMEM(back.shape, jnp.bfloat16), pltpu.SemaphoreType.DMA((N_SEQ,))],
        compiler_params=params(44), name="attend",
    )(lo, hi, got, gain, ids)


def windows(ids):
    first = ids[:, 0::BQ]
    last = ids[:, BQ - 1::BQ]
    lo = jnp.sum((ids[0][:, None] < first).astype(jnp.int32), axis=0)
    hi = jnp.sum((ids[0][:, None] <= last).astype(jnp.int32), axis=0)
    return (lo, hi)


def local(q_in, k_in, v_in, gain_q, gain_k, clip_ids):
    place = lax.axis_index("dp") % 8
    turn = (lax.axis_index("dp") // 8).astype(jnp.int32)[None]
    inv = shape((TOK, HD), jnp.float32)
    three = pltpu.VMEM((3, TOK, WIDTH), jnp.bfloat16)

    row = spread(jnp.stack([gain_q, gain_k]))[None]
    rows = jnp.where(lax.broadcasted_iota(jnp.int32, (8, HD), 0) == place, row, 0.0)

    pay, inv_q, inv_k, mark = pl.pallas_call(
        pack_kernel,
        out_shape=[shape((N_SEQ, BODY + EXTRA, HD)), inv, inv, shape((8, HD), jnp.float32)],
        in_specs=[SCALARS] + [THERE] * 3, out_specs=[THERE, HERE, HERE, HERE],
        scratch_shapes=[three, pltpu.VMEM((EXTRA, HD), jnp.bfloat16),
                        pltpu.SemaphoreType.DMA((3 * CUTS,)), pltpu.SemaphoreType.DMA((3 * H + N_SEQ,))],
        compiler_params=params(62), name="pack",
    )(turn, q_in, k_in, v_in)
    got = lax.all_to_all(pay, "seq", 0, 0, tiled=True)
    rows = lax.ppermute(over_y(hold(over_z(rows), mark)), ("dp", "seq"), around(-1))
    lo, hi = windows(clip_ids)
    pay, part = attend_call(lo, hi, got, rows, clip_ids)

    blocks = [list(range(b, b + 8)) for b in range(0, 64, 8)]
    part = lax.all_to_all(part, "dp", 0, 0, axis_index_groups=blocks, tiled=True)
    part = jnp.sum(part, axis=0, keepdims=True)
    pay, part = lax.optimization_barrier((pay, part))
    got = lax.all_to_all(pay, "seq", 0, 0, tiled=True)
    part = hold(part, part)
    part = over_x(over_core(lax.ppermute(part, ("dp", "seq"), around(1))))[0]

    out = shape((TOK, WIDTH))
    d_q, d_k, d_v = pl.pallas_call(
        final_kernel, out_shape=[out] * 3,
        in_specs=[SCALARS] + [HERE] * 5, out_specs=[THERE] * 3,
        scratch_shapes=[three, pltpu.SemaphoreType.DMA((3,))],
        compiler_params=params(16), name="final",
        cost_estimate=pl.CostEstimate(flops=1 << 34, bytes_accessed=1 << 25, transcendentals=0),
    )(turn, q_in, k_in, inv_q, inv_k, got)
    return (d_q, d_k, d_v, part[0:SHARD], part[64:64 + SHARD])


def solution(mesh):
    rows = P(("dp", "seq"), None)
    return jax.shard_map(
        local, mesh=mesh,
        in_specs=(rows, rows, rows, P("dp"), P("dp"), P("dp", None)),
        out_specs=(rows, rows, rows, P("dp"), P("dp")), check_vma=False)
```

```python
import jax
import jax.numpy as jnp
from jax import lax
from jax.experimental import pallas as pl
from jax.experimental.pallas import tpu as pltpu
from jax.sharding import PartitionSpec as P

H = 24
HD = 128
TOK = 128
N_SEQ = 8
HEADS = H // N_SEQ
G = TOK * N_SEQ
WIDTH = H * HD
BQ = 256
PAIR = 1
WINDOWS = (384, 512, 640, 768, 896, 1024)
EXTRA = 16
BODY = 3 * TOK * HEADS
EPS = 1e-06
SCALE = HD ** (-0.5)
LOG2E = 1.4426950408889634
SHARD = 48
CUTS = 4


def split3(x):
    hi = x.astype(jnp.bfloat16).astype(jnp.float32)
    mid = (x - hi).astype(jnp.bfloat16).astype(jnp.float32)
    return (hi, mid, x - hi - mid)


def extra_rows(rows, size):
    at = lax.broadcasted_iota(jnp.int32, (size, HD), 0)
    out = jnp.zeros((size, HD), jnp.float32)
    for index, piece in enumerate([piece for row in rows for piece in split3(row)]):
        out = jnp.where(at == index, piece, out)
    return out.astype(jnp.bfloat16)


def join3(extra, n):
    x = extra[3 * n:3 * n + 3]
    return (x[0:1] + x[1:2]) + x[2:3]


def column(row):
    return jnp.transpose(jnp.broadcast_to(row, (HD, HD)))


def body(c, n):
    return slice((c * 3 + n) * TOK, (c * 3 + n + 1) * TOK)


def pack_kernel(turn_ref, q_ref, k_ref, v_ref, pay_ref, inv_q_ref, inv_k_ref, mark_ref, held, extra, load_sems, sems):
    wide = WIDTH // CUTS
    loads = []
    for t in range(CUTS):
        cols = slice(t * wide, (t + 1) * wide)
        for n, ref in enumerate((q_ref, k_ref, v_ref)):
            loads.append(pltpu.make_async_copy(ref.at[:, cols], held.at[n, :, cols], load_sems.at[len(loads)]))
            loads[-1].start()
    copies = []
    for t in range(CUTS):
        for n in range(3):
            loads[3 * t + n].wait()
            for h in range(t * H // CUTS, (t + 1) * H // CUTS):
                dest = (h // HEADS + N_SEQ - turn_ref[0]) % N_SEQ
                copies.append(pltpu.make_async_copy(
                    held.at[n, :, h * HD:(h + 1) * HD], pay_ref.at[dest, body(h % HEADS, n)], sems.at[len(copies)]))
                copies[-1].start()
    rows = []
    for n, inv_ref in enumerate((inv_q_ref, inv_k_ref)):
        total = jnp.zeros((TOK, HD), jnp.float32)
        for h in range(H):
            x = held[n, :, h * HD:(h + 1) * HD].astype(jnp.float32)
            total = total + x * x
        inv = lax.rsqrt(jnp.sum(total, axis=1, keepdims=True) * (1.0 / WIDTH) + EPS)
        inv = jnp.broadcast_to(inv, (TOK, HD))
        inv_ref[...] = inv
        rows.append(jnp.transpose(inv)[0:1])
    mark_ref[...] = jnp.zeros_like(mark_ref)
    extra[...] = extra_rows(rows, EXTRA)
    for s in range(N_SEQ):
        copies.append(pltpu.make_async_copy(extra, pay_ref.at[s, BODY:], sems.at[len(copies)]))
        copies[-1].start()
    for copy in copies:
        copy.wait()


def nt(a, b):
    return lax.dot_general(a, b, (((1,), (1,)), ((), ())), preferred_element_type=jnp.float32)


def nn(a, b):
    return jnp.dot(a, b, preferred_element_type=jnp.float32)


def gather_lanes(rows):
    lane = lax.broadcasted_iota(jnp.int32, (8, HD), 1)
    out = []
    for n in range(2):
        part = jnp.where(lane < SHARD, pltpu.roll(rows, (HD - 64 * n) % HD, 1), 0.0)
        part = jnp.concatenate([part, jnp.zeros((8, (HEADS - 1) * HD), jnp.float32)], axis=1)
        total = part[0:1]
        for j in range(1, 8):
            total = total + pltpu.roll(part, SHARD * j, 1)[j:j + 1]
        out.append(total)
    return out


def spread_lanes(wide):
    lane = lax.broadcasted_iota(jnp.int32, (8, HD), 1)
    at = lax.broadcasted_iota(jnp.int32, (8, HD), 0)
    out = jnp.zeros((8, HD), jnp.float32)
    for n in range(2):
        x = jnp.broadcast_to(wide[n], (8, HEADS * HD))
        for j in range(8):
            part = pltpu.roll(x, (HEADS * HD - SHARD * j) % (HEADS * HD), 1)[:, 0:HD]
            part = pltpu.roll(part, 64 * n, 1)
            keep = jnp.logical_and(at == j, jnp.logical_and(lane >= 64 * n, lane < 64 * n + SHARD))
            out = jnp.where(keep, part, out)
    return out


def attend_kernel(lo_ref, hi_ref, pay_ref, gain_ref, ids_ref, out_ref, dg_ref,
                  qn, kn, vv, dq, acc_k, acc_v, mq, mk, outs, sems):
    for j in range(N_SEQ):
        extra = pay_ref[j, BODY:].astype(jnp.float32)
        at = slice(j * TOK, (j + 1) * TOK)
        mq[at] = column(join3(extra, 0))
        mk[at] = column(join3(extra, 1))
    wide = gather_lanes(gain_ref[...])
    gains = [[wide[n][:, c * HD:(c + 1) * HD] for n in range(2)] for c in range(HEADS)]
    extra = extra_rows([row for pair in gains for row in pair], 2 * EXTRA)
    for j in range(N_SEQ):
        outs[j, BODY:] = extra

    def hats(c, j):
        at = slice(j * TOK, (j + 1) * TOK)
        return (pay_ref[j, body(c, 0)].astype(jnp.float32) * mq[at],
                pay_ref[j, body(c, 1)].astype(jnp.float32) * mk[at])

    for c in range(HEADS):
        for j in range(N_SEQ):
            q, k = hats(c, j)
            at = slice(j * TOK, (j + 1) * TOK)
            qn[c, at] = (q * gains[c][0]).astype(jnp.bfloat16)
            kn[c, at] = (k * gains[c][1]).astype(jnp.bfloat16)
            vv[c, at] = pay_ref[j, body(c, 2)]
    acc_k[...] = jnp.zeros_like(acc_k)
    acc_v[...] = jnp.zeros_like(acc_v)

    def blocks(b, first, width):
        units = [(t, c) for t in range(PAIR) for c in range(HEADS)]
        start = [pl.multiple_of(f, TOK) for f in first]
        rows = [pl.ds(pl.multiple_of((b * PAIR + t) * BQ, BQ), BQ) for t in range(PAIR)]
        keys = [pl.ds(f, width) for f in start]
        same = []
        for t in range(PAIR):
            own = [column(ids_ref[:, pl.ds(pl.multiple_of((b * PAIR + t) * BQ + r, HD), HD)])[:, 0:1]
                   for r in range(0, BQ, HD)]
            same.append(jnp.concatenate(own, axis=0) == ids_ref[:, keys[t]])
        qb = {(t, c): qn[c, rows[t]] for t, c in units}
        kb = {(t, c): kn[c, keys[t]] for t, c in units}
        vb = {(t, c): vv[c, keys[t]] for t, c in units}
        val = {}

        def score(u):
            val["s", u] = nt(qb[u], kb[u])

        def soft(u):
            s = jnp.where(same[u[0]], val["s", u], -1e30)
            top = jnp.max(s, axis=1, keepdims=True)
            e = jnp.exp2((s - top) * (SCALE * LOG2E))
            val["p", u] = e * (1.0 / jnp.sum(e, axis=1, keepdims=True))
            val["pb", u] = val["p", u].astype(jnp.bfloat16)

        def mix(u):
            val["a", u] = nn(val["pb", u], vb[u]).astype(jnp.bfloat16)

        def back(u):
            val["dp", u] = nt(val["a", u], vb[u])

        def less(u):
            p, dp = val["p", u], val["dp", u]
            delta = jnp.sum(p * dp, axis=1, keepdims=True)
            val["ds", u] = (p * (dp - delta) * SCALE).astype(jnp.bfloat16)

        def values(u):
            acc_v[u[1], :, keys[u[0]]] += nn(jnp.transpose(val["a", u]), val["pb", u])

        def grads(u):
            dq[u[1], rows[u[0]]] = nn(val["ds", u], kb[u]).astype(jnp.bfloat16)
            acc_k[u[1], :, keys[u[0]]] += nn(jnp.transpose(qb[u]), val["ds", u])

        for stage in (score, soft, mix, back, less, values, grads):
            for u in units:
                stage(u)

    def step(b, carry):
        low = [lo_ref[b * PAIR + t] // TOK * TOK for t in range(PAIR)]
        span = hi_ref[b * PAIR] - low[0]
        for t in range(1, PAIR):
            span = jnp.maximum(span, hi_ref[b * PAIR + t] - low[t])
        done = None
        for width in WINDOWS:
            fits = span <= width
            now = fits if done is None else jnp.logical_and(fits, jnp.logical_not(done))
            done = fits

            @pl.when(now)
            def _():
                blocks(b, [jnp.minimum(f, G - width) for f in low], width)
        return carry

    lax.fori_loop(0, G // BQ // PAIR, step, 0)

    copies = []
    for j in range(N_SEQ):
        at = slice(j * TOK, (j + 1) * TOK)
        for c in range(HEADS):
            outs[j, body(c, 0)] = dq[c, at]
            outs[j, body(c, 1)] = jnp.transpose(acc_k[c, :, at].astype(jnp.bfloat16))
            outs[j, body(c, 2)] = jnp.transpose(acc_v[c, :, at].astype(jnp.bfloat16))
        copies.append(pltpu.make_async_copy(outs.at[j], out_ref.at[j], sems.at[j]))
        copies[j].start()
    wide = [[], []]
    for c in range(HEADS):
        sums = [jnp.zeros((TOK, HD), jnp.float32)] * 2
        for j in range(N_SEQ):
            hat = hats(c, j)
            sums = [sums[n] + outs[j, body(c, n)].astype(jnp.float32) * hat[n] for n in range(2)]
        for n in range(2):
            wide[n].append(jnp.sum(sums[n], axis=0, keepdims=True))
    dg_ref[...] = spread_lanes([jnp.concatenate(rows, axis=1) for rows in wide])
    for copy in copies:
        copy.wait()


def final_kernel(turn_ref, q_ref, k_ref, inv_q_ref, inv_k_ref, pay_ref, dq_ref, dk_ref, dv_ref, outs, sems):
    src = [(g + N_SEQ - turn_ref[0]) % N_SEQ for g in range(N_SEQ)]
    pairs = [(g, c, slice((g * HEADS + c) * HD, (g * HEADS + c + 1) * HD))
             for g in range(N_SEQ) for c in range(HEADS)]
    copies = []

    def send(n, ref):
        copies.append(pltpu.make_async_copy(outs.at[n], ref, sems.at[n]))
        copies[-1].start()

    for g, c, cols in pairs:
        outs[2, :, cols] = pay_ref[src[g], body(c, 2)]
    send(2, dv_ref)
    extras = [pay_ref[src[g], BODY:].astype(jnp.float32) for g in range(N_SEQ)]
    for n, (ref, inv_ref, out_ref) in enumerate(((q_ref, inv_q_ref, dq_ref), (k_ref, inv_k_ref, dk_ref))):
        inv = inv_ref[...]

        def parts(g, c, cols):
            dhat = pay_ref[src[g], body(c, n)].astype(jnp.float32) * join3(extras[g], 2 * c + n)
            return (dhat, ref[:, cols].astype(jnp.float32) * inv)

        total = jnp.zeros((TOK, HD), jnp.float32)
        for pair in pairs:
            dhat, hat = parts(*pair)
            total = total + dhat * hat
        mean = jnp.sum(total, axis=1, keepdims=True) * (1.0 / WIDTH)
        for pair in pairs:
            dhat, hat = parts(*pair)
            outs[n, :, pair[2]] = (inv * (dhat - hat * mean)).astype(jnp.bfloat16)
        send(n, out_ref)
    for copy in copies:
        copy.wait()


def hold_kernel(x_ref, after_ref, out_ref):
    out_ref[...] = x_ref[...]


def hold(x, after):
    return pl.pallas_call(
        hold_kernel, out_shape=shape(x.shape, jnp.float32),
        in_specs=[HERE, HERE], out_specs=HERE,
        compiler_params=params(1), name="hold", cost_estimate=pl.CostEstimate(flops=1 << 36, bytes_accessed=1 << 27, transcendentals=0),
    )(x, after)


def shape(dims, dtype=jnp.bfloat16):
    return jax.ShapeDtypeStruct(dims, dtype)


def params(mib):
    return pltpu.CompilerParams(vmem_limit_bytes=mib * 1024 * 1024)


HERE = pl.BlockSpec(memory_space=pltpu.VMEM)
THERE = pl.BlockSpec(memory_space=pltpu.HBM)
SCALARS = pl.BlockSpec(memory_space=pltpu.SMEM)


def around(way):
    return [((b * 8 + i) * 8 + s, ((b + way * s) % 8 * 8 + i) * 8 + s)
            for b in range(8) for i in range(8) for s in range(8)]


def sum_four(x, axis, pairs):
    one, two, three = (lax.ppermute(x, axis, pairs(k)) for k in (1, 2, 3))
    return (x + two) + (one + three)


def over_z(x):
    return x + lax.ppermute(x, "dp", [(d, d ^ 4) for d in range(64)])


def over_y(x):
    return sum_four(x, "dp", lambda k: [(d, d // 4 * 4 + (d + k) % 4) for d in range(64)])


def over_core(x):
    return x + lax.ppermute(x, "seq", [(s, s ^ 1) for s in range(8)])


def over_x(x):
    return sum_four(x, "seq", lambda k: [(s, (s + 2 * k) % 8) for s in range(8)])


def spread(pair):
    pad = jnp.zeros(pair.shape[:-2] + (16,), jnp.float32)
    return jnp.concatenate([pair[..., 0, :], pad, pair[..., 1, :], pad], axis=-1)


def attend_call(lo, hi, got, gain, ids):
    back = shape((N_SEQ, BODY + 2 * EXTRA, HD))
    half = pltpu.VMEM((HEADS, G, HD), jnp.bfloat16)
    full = pltpu.VMEM((G, HD), jnp.float32)
    turn = pltpu.VMEM((HEADS, HD, G), jnp.float32)
    return pl.pallas_call(
        attend_kernel, out_shape=[back, shape((8, HD), jnp.float32)],
        in_specs=[SCALARS, SCALARS, HERE, HERE, HERE], out_specs=[THERE, HERE],
        scratch_shapes=[half] * 4 + [turn] * 2 + [full] * 2 + [
            pltpu.VMEM(back.shape, jnp.bfloat16), pltpu.SemaphoreType.DMA((N_SEQ,))],
        compiler_params=params(44), name="attend",
    )(lo, hi, got, gain, ids)


def windows(ids):
    first = ids[:, 0::BQ]
    last = ids[:, BQ - 1::BQ]
    lo = jnp.sum((ids[0][:, None] < first).astype(jnp.int32), axis=0)
    hi = jnp.sum((ids[0][:, None] <= last).astype(jnp.int32), axis=0)
    return (lo, hi)


def local(q_in, k_in, v_in, gain_q, gain_k, clip_ids):
    place = lax.axis_index("dp") % 8
    turn = (lax.axis_index("dp") // 8).astype(jnp.int32)[None]
    inv = shape((TOK, HD), jnp.float32)
    three = pltpu.VMEM((3, TOK, WIDTH), jnp.bfloat16)

    row = spread(jnp.stack([gain_q, gain_k]))[None]
    rows = jnp.where(lax.broadcasted_iota(jnp.int32, (8, HD), 0) == place, row, 0.0)

    pay, inv_q, inv_k, mark = pl.pallas_call(
        pack_kernel,
        out_shape=[shape((N_SEQ, BODY + EXTRA, HD)), inv, inv, shape((8, HD), jnp.float32)],
        in_specs=[SCALARS] + [THERE] * 3, out_specs=[THERE, HERE, HERE, HERE],
        scratch_shapes=[three, pltpu.VMEM((EXTRA, HD), jnp.bfloat16),
                        pltpu.SemaphoreType.DMA((3 * CUTS,)), pltpu.SemaphoreType.DMA((3 * H + N_SEQ,))],
        compiler_params=params(62), name="pack",
    )(turn, q_in, k_in, v_in)
    got = lax.all_to_all(pay, "seq", 0, 0, tiled=True)
    rows = lax.ppermute(over_y(hold(over_z(rows), mark)), ("dp", "seq"), around(-1))
    lo, hi = windows(clip_ids)
    pay, part = attend_call(lo, hi, got, rows, clip_ids)

    got = lax.all_to_all(pay, "seq", 0, 0, tiled=True)
    part = over_y(hold(over_z(part), part))
    part = lax.dynamic_slice_in_dim(part, place, 1, 0)
    part = lax.ppermute(part, ("dp", "seq"), around(1))
    part, got = lax.optimization_barrier((part, got))
    part = lax.all_to_all(jnp.broadcast_to(part, (N_SEQ, HD))[:, None], "seq", 0, 0, tiled=True)
    part = jnp.sum(part, axis=(0, 1))

    out = shape((TOK, WIDTH))
    d_q, d_k, d_v = pl.pallas_call(
        final_kernel, out_shape=[out] * 3,
        in_specs=[SCALARS] + [HERE] * 5, out_specs=[THERE] * 3,
        scratch_shapes=[three, pltpu.SemaphoreType.DMA((3,))],
        compiler_params=params(16), name="final",
        cost_estimate=pl.CostEstimate(flops=1 << 34, bytes_accessed=1 << 25, transcendentals=0),
    )(turn, q_in, k_in, inv_q, inv_k, got)
    return (d_q, d_k, d_v, part[0:SHARD], part[64:64 + SHARD])


def solution(mesh):
    rows = P(("dp", "seq"), None)
    return jax.shard_map(
        local, mesh=mesh,
        in_specs=(rows, rows, rows, P("dp"), P("dp"), P("dp", None)),
        out_specs=(rows, rows, rows, P("dp"), P("dp")), check_vma=False)
```

```python
import jax
import jax.numpy as jnp
from jax import lax
from jax.experimental import pallas as pl
from jax.experimental.pallas import tpu as pltpu
from jax.sharding import PartitionSpec as P

H = 24
HD = 128
TOK = 128
N_SEQ = 8
HEADS = H // N_SEQ
G = TOK * N_SEQ
WIDTH = H * HD
BQ = 256
PAIR = 1
WINDOWS = (384, 512, 640, 768, 896, 1024)
EXTRA = 16
BODY = 3 * TOK * HEADS
EPS = 1e-06
SCALE = HD ** (-0.5)
LOG2E = 1.4426950408889634
SHARD = 48
CUTS = 4


def split3(x):
    hi = x.astype(jnp.bfloat16).astype(jnp.float32)
    mid = (x - hi).astype(jnp.bfloat16).astype(jnp.float32)
    return (hi, mid, x - hi - mid)


def extra_rows(rows, size):
    at = lax.broadcasted_iota(jnp.int32, (size, HD), 0)
    out = jnp.zeros((size, HD), jnp.float32)
    for index, piece in enumerate([piece for row in rows for piece in split3(row)]):
        out = jnp.where(at == index, piece, out)
    return out.astype(jnp.bfloat16)


def join3(extra, n):
    x = extra[3 * n:3 * n + 3]
    return (x[0:1] + x[1:2]) + x[2:3]


def column(row):
    return jnp.transpose(jnp.broadcast_to(row, (HD, HD)))


def body(c, n):
    return slice((c * 3 + n) * TOK, (c * 3 + n + 1) * TOK)


def pack_kernel(turn_ref, q_ref, k_ref, v_ref, gain_q_ref, gain_k_ref, pay_ref, inv_q_ref, inv_k_ref, rows_ref,
                held, extra, one, two, load_sems, sems):
    wide = WIDTH // CUTS
    loads = []
    for t in range(CUTS):
        cols = slice(t * wide, (t + 1) * wide)
        for n, ref in enumerate((q_ref, k_ref, v_ref)):
            loads.append(pltpu.make_async_copy(ref.at[:, cols], held.at[n, :, cols], load_sems.at[len(loads)]))
            loads[-1].start()
    copies = []
    for t in range(CUTS):
        for n in range(3):
            loads[3 * t + n].wait()
            for h in range(t * H // CUTS, (t + 1) * H // CUTS):
                dest = (h // HEADS + N_SEQ - turn_ref[0] // 8) % N_SEQ
                copies.append(pltpu.make_async_copy(
                    held.at[n, :, h * HD:(h + 1) * HD], pay_ref.at[dest, body(h % HEADS, n)], sems.at[len(copies)]))
                copies[-1].start()
    rows = []
    for n, inv_ref in enumerate((inv_q_ref, inv_k_ref)):
        total = jnp.zeros((TOK, HD), jnp.float32)
        for h in range(H):
            x = held[n, :, h * HD:(h + 1) * HD].astype(jnp.float32)
            total = total + x * x
        inv = lax.rsqrt(jnp.sum(total, axis=1, keepdims=True) * (1.0 / WIDTH) + EPS)
        inv = jnp.broadcast_to(inv, (TOK, HD))
        inv_ref[...] = inv
        rows.append(jnp.transpose(inv)[0:1])
    one[...] = jnp.zeros_like(one)
    two[...] = jnp.zeros_like(two)
    one[0:1, 0:SHARD] = gain_q_ref[...]
    two[0:1, 0:SHARD] = gain_k_ref[...]
    row = (one[...] + pltpu.roll(two[...], 64, 1))[0:1]
    rows_ref[...] = jnp.where(lax.broadcasted_iota(jnp.int32, (8, HD), 0) == turn_ref[0] % 8, row, 0.0)
    extra[...] = extra_rows(rows, EXTRA)
    for s in range(N_SEQ):
        copies.append(pltpu.make_async_copy(extra, pay_ref.at[s, BODY:], sems.at[len(copies)]))
        copies[-1].start()
    for copy in copies:
        copy.wait()


def nt(a, b):
    return lax.dot_general(a, b, (((1,), (1,)), ((), ())), preferred_element_type=jnp.float32)


def nn(a, b):
    return jnp.dot(a, b, preferred_element_type=jnp.float32)


def gather_lanes(rows):
    lane = lax.broadcasted_iota(jnp.int32, (8, HD), 1)
    out = []
    for n in range(2):
        part = jnp.where(lane < SHARD, pltpu.roll(rows, (HD - 64 * n) % HD, 1), 0.0)
        part = jnp.concatenate([part, jnp.zeros((8, (HEADS - 1) * HD), jnp.float32)], axis=1)
        total = part[0:1]
        for j in range(1, 8):
            total = total + pltpu.roll(part, SHARD * j, 1)[j:j + 1]
        out.append(total)
    return out


def spread_lanes(wide):
    lane = lax.broadcasted_iota(jnp.int32, (8, HD), 1)
    at = lax.broadcasted_iota(jnp.int32, (8, HD), 0)
    out = jnp.zeros((8, HD), jnp.float32)
    for n in range(2):
        x = jnp.broadcast_to(wide[n], (8, HEADS * HD))
        for j in range(8):
            part = pltpu.roll(x, (HEADS * HD - SHARD * j) % (HEADS * HD), 1)[:, 0:HD]
            part = pltpu.roll(part, 64 * n, 1)
            keep = jnp.logical_and(at == j, jnp.logical_and(lane >= 64 * n, lane < 64 * n + SHARD))
            out = jnp.where(keep, part, out)
    return out


def attend_kernel(lo_ref, hi_ref, pay_ref, gain_ref, ids_ref, out_ref, dg_ref,
                  qn, kn, vv, dq, acc_k, acc_v, mq, mk, outs, sems):
    for j in range(N_SEQ):
        extra = pay_ref[j, BODY:].astype(jnp.float32)
        at = slice(j * TOK, (j + 1) * TOK)
        mq[at] = column(join3(extra, 0))
        mk[at] = column(join3(extra, 1))
    wide = gather_lanes(gain_ref[...])
    gains = [[wide[n][:, c * HD:(c + 1) * HD] for n in range(2)] for c in range(HEADS)]
    extra = extra_rows([row for pair in gains for row in pair], 2 * EXTRA)
    for j in range(N_SEQ):
        outs[j, BODY:] = extra

    def hats(c, j):
        at = slice(j * TOK, (j + 1) * TOK)
        return (pay_ref[j, body(c, 0)].astype(jnp.float32) * mq[at],
                pay_ref[j, body(c, 1)].astype(jnp.float32) * mk[at])

    for c in range(HEADS):
        for j in range(N_SEQ):
            q, k = hats(c, j)
            at = slice(j * TOK, (j + 1) * TOK)
            qn[c, at] = (q * gains[c][0]).astype(jnp.bfloat16)
            kn[c, at] = (k * gains[c][1]).astype(jnp.bfloat16)
            vv[c, at] = pay_ref[j, body(c, 2)]
    acc_k[...] = jnp.zeros_like(acc_k)
    acc_v[...] = jnp.zeros_like(acc_v)

    def blocks(b, first, width):
        units = [(t, c) for t in range(PAIR) for c in range(HEADS)]
        start = [pl.multiple_of(f, TOK) for f in first]
        rows = [pl.ds(pl.multiple_of((b * PAIR + t) * BQ, BQ), BQ) for t in range(PAIR)]
        keys = [pl.ds(f, width) for f in start]
        same = []
        for t in range(PAIR):
            own = [column(ids_ref[:, pl.ds(pl.multiple_of((b * PAIR + t) * BQ + r, HD), HD)])[:, 0:1]
                   for r in range(0, BQ, HD)]
            same.append(jnp.concatenate(own, axis=0) == ids_ref[:, keys[t]])
        qb = {(t, c): qn[c, rows[t]] for t, c in units}
        kb = {(t, c): kn[c, keys[t]] for t, c in units}
        vb = {(t, c): vv[c, keys[t]] for t, c in units}
        val = {}

        def score(u):
            val["s", u] = nt(qb[u], kb[u])

        def soft(u):
            s = jnp.where(same[u[0]], val["s", u], -1e30)
            top = jnp.max(s, axis=1, keepdims=True)
            e = jnp.exp2((s - top) * (SCALE * LOG2E))
            val["p", u] = e * (1.0 / jnp.sum(e, axis=1, keepdims=True))
            val["pb", u] = val["p", u].astype(jnp.bfloat16)

        def mix(u):
            val["a", u] = nn(val["pb", u], vb[u]).astype(jnp.bfloat16)

        def back(u):
            val["dp", u] = nt(val["a", u], vb[u])

        def less(u):
            p, dp = val["p", u], val["dp", u]
            delta = jnp.sum(p * dp, axis=1, keepdims=True)
            val["ds", u] = (p * (dp - delta) * SCALE).astype(jnp.bfloat16)

        def values(u):
            acc_v[u[1], :, keys[u[0]]] += nn(jnp.transpose(val["a", u]), val["pb", u])

        def grads(u):
            dq[u[1], rows[u[0]]] = nn(val["ds", u], kb[u]).astype(jnp.bfloat16)
            acc_k[u[1], :, keys[u[0]]] += nn(jnp.transpose(qb[u]), val["ds", u])

        for stage in (score, soft, mix, back, less, values, grads):
            for u in units:
                stage(u)

    def step(b, carry):
        low = [lo_ref[b * PAIR + t] // TOK * TOK for t in range(PAIR)]
        span = hi_ref[b * PAIR] - low[0]
        for t in range(1, PAIR):
            span = jnp.maximum(span, hi_ref[b * PAIR + t] - low[t])
        done = None
        for width in WINDOWS:
            fits = span <= width
            now = fits if done is None else jnp.logical_and(fits, jnp.logical_not(done))
            done = fits

            @pl.when(now)
            def _():
                blocks(b, [jnp.minimum(f, G - width) for f in low], width)
        return carry

    lax.fori_loop(0, G // BQ // PAIR, step, 0)

    copies = []
    for j in range(N_SEQ):
        at = slice(j * TOK, (j + 1) * TOK)
        for c in range(HEADS):
            outs[j, body(c, 0)] = dq[c, at]
            outs[j, body(c, 1)] = jnp.transpose(acc_k[c, :, at].astype(jnp.bfloat16))
            outs[j, body(c, 2)] = jnp.transpose(acc_v[c, :, at].astype(jnp.bfloat16))
        copies.append(pltpu.make_async_copy(outs.at[j], out_ref.at[j], sems.at[j]))
        copies[j].start()
    wide = [[], []]
    for c in range(HEADS):
        sums = [jnp.zeros((TOK, HD), jnp.float32)] * 2
        for j in range(N_SEQ):
            hat = hats(c, j)
            sums = [sums[n] + outs[j, body(c, n)].astype(jnp.float32) * hat[n] for n in range(2)]
        for n in range(2):
            wide[n].append(jnp.sum(sums[n], axis=0, keepdims=True))
    dg_ref[...] = spread_lanes([jnp.concatenate(rows, axis=1) for rows in wide])
    for copy in copies:
        copy.wait()


def final_kernel(turn_ref, q_ref, k_ref, inv_q_ref, inv_k_ref, pay_ref, dq_ref, dk_ref, dv_ref, outs, sems):
    src = [(g + N_SEQ - turn_ref[0] // 8) % N_SEQ for g in range(N_SEQ)]
    pairs = [(g, c, slice((g * HEADS + c) * HD, (g * HEADS + c + 1) * HD))
             for g in range(N_SEQ) for c in range(HEADS)]
    copies = []

    def send(n, ref):
        copies.append(pltpu.make_async_copy(outs.at[n], ref, sems.at[n]))
        copies[-1].start()

    for g, c, cols in pairs:
        outs[2, :, cols] = pay_ref[src[g], body(c, 2)]
    send(2, dv_ref)
    extras = [pay_ref[src[g], BODY:].astype(jnp.float32) for g in range(N_SEQ)]
    for n, (ref, inv_ref, out_ref) in enumerate(((q_ref, inv_q_ref, dq_ref), (k_ref, inv_k_ref, dk_ref))):
        inv = inv_ref[...]

        def parts(g, c, cols):
            dhat = pay_ref[src[g], body(c, n)].astype(jnp.float32) * join3(extras[g], 2 * c + n)
            return (dhat, ref[:, cols].astype(jnp.float32) * inv)

        total = jnp.zeros((TOK, HD), jnp.float32)
        for pair in pairs:
            dhat, hat = parts(*pair)
            total = total + dhat * hat
        mean = jnp.sum(total, axis=1, keepdims=True) * (1.0 / WIDTH)
        for pair in pairs:
            dhat, hat = parts(*pair)
            outs[n, :, pair[2]] = (inv * (dhat - hat * mean)).astype(jnp.bfloat16)
        send(n, out_ref)
    for copy in copies:
        copy.wait()


def hold_kernel(x_ref, after_ref, out_ref):
    out_ref[...] = x_ref[...]


def hold(x, after):
    return pl.pallas_call(
        hold_kernel, out_shape=shape(x.shape, jnp.float32),
        in_specs=[HERE, HERE], out_specs=HERE,
        compiler_params=params(1), name="hold", cost_estimate=pl.CostEstimate(flops=1 << 36, bytes_accessed=1 << 27, transcendentals=0),
    )(x, after)


def shape(dims, dtype=jnp.bfloat16):
    return jax.ShapeDtypeStruct(dims, dtype)


def params(mib):
    return pltpu.CompilerParams(vmem_limit_bytes=mib * 1024 * 1024)


HERE = pl.BlockSpec(memory_space=pltpu.VMEM)
THERE = pl.BlockSpec(memory_space=pltpu.HBM)
SCALARS = pl.BlockSpec(memory_space=pltpu.SMEM)


def around(way):
    return [((b * 8 + i) * 8 + s, ((b + way * s) % 8 * 8 + i) * 8 + s)
            for b in range(8) for i in range(8) for s in range(8)]


def sum_four(x, axis, pairs):
    one, two, three = (lax.ppermute(x, axis, pairs(k)) for k in (1, 2, 3))
    return (x + two) + (one + three)


def over_z(x):
    return x + lax.ppermute(x, "dp", [(d, d ^ 4) for d in range(64)])


def over_y(x):
    return sum_four(x, "dp", lambda k: [(d, d // 4 * 4 + (d + k) % 4) for d in range(64)])


def over_core(x):
    return x + lax.ppermute(x, "seq", [(s, s ^ 1) for s in range(8)])


def over_x(x):
    return sum_four(x, "seq", lambda k: [(s, (s + 2 * k) % 8) for s in range(8)])


def attend_call(lo, hi, got, gain, ids):
    back = shape((N_SEQ, BODY + 2 * EXTRA, HD))
    half = pltpu.VMEM((HEADS, G, HD), jnp.bfloat16)
    full = pltpu.VMEM((G, HD), jnp.float32)
    turn = pltpu.VMEM((HEADS, HD, G), jnp.float32)
    return pl.pallas_call(
        attend_kernel, out_shape=[back, shape((8, HD), jnp.float32)],
        in_specs=[SCALARS, SCALARS, HERE, HERE, HERE], out_specs=[THERE, HERE],
        scratch_shapes=[half] * 4 + [turn] * 2 + [full] * 2 + [
            pltpu.VMEM(back.shape, jnp.bfloat16), pltpu.SemaphoreType.DMA((N_SEQ,))],
        compiler_params=params(44), name="attend",
    )(lo, hi, got, gain, ids)


def windows(ids):
    first = ids[:, 0::BQ]
    last = ids[:, BQ - 1::BQ]
    lo = jnp.sum((ids[0][:, None] < first).astype(jnp.int32), axis=0)
    hi = jnp.sum((ids[0][:, None] <= last).astype(jnp.int32), axis=0)
    return (lo, hi)


def local(q_in, k_in, v_in, gain_q, gain_k, clip_ids):
    place = lax.axis_index("dp") % 8
    turn = lax.axis_index("dp").astype(jnp.int32)[None]
    inv = shape((TOK, HD), jnp.float32)
    three = pltpu.VMEM((3, TOK, WIDTH), jnp.bfloat16)
    row = pltpu.VMEM((8, HD), jnp.float32)

    pay, inv_q, inv_k, rows = pl.pallas_call(
        pack_kernel,
        out_shape=[shape((N_SEQ, BODY + EXTRA, HD)), inv, inv, shape((8, HD), jnp.float32)],
        in_specs=[SCALARS] + [THERE] * 3 + [HERE] * 2, out_specs=[THERE, HERE, HERE, HERE],
        scratch_shapes=[three, pltpu.VMEM((EXTRA, HD), jnp.bfloat16), row, row,
                        pltpu.SemaphoreType.DMA((3 * CUTS,)), pltpu.SemaphoreType.DMA((3 * H + N_SEQ,))],
        compiler_params=params(62), name="pack",
    )(turn, q_in, k_in, v_in, gain_q[None], gain_k[None])
    got = lax.all_to_all(pay, "seq", 0, 0, tiled=True)
    rows = lax.ppermute(over_y(hold(over_z(rows), rows)), ("dp", "seq"), around(-1))
    lo, hi = windows(clip_ids)
    pay, part = attend_call(lo, hi, got, rows, clip_ids)

    got = lax.all_to_all(pay, "seq", 0, 0, tiled=True)
    part = over_y(over_z(hold(part, part)))
    part = lax.dynamic_slice_in_dim(part, place, 1, 0)
    part = lax.ppermute(part, ("dp", "seq"), around(1))
    part = jnp.broadcast_to(part, (N_SEQ, HD))[:, None]
    part, got = lax.optimization_barrier((part, got))
    part = lax.all_to_all(part, "seq", 0, 0, tiled=True)
    part = jnp.sum(part, axis=(0, 1))

    out = shape((TOK, WIDTH))
    d_q, d_k, d_v = pl.pallas_call(
        final_kernel, out_shape=[out] * 3,
        in_specs=[SCALARS] + [HERE] * 5, out_specs=[THERE] * 3,
        scratch_shapes=[three, pltpu.SemaphoreType.DMA((3,))],
        compiler_params=params(16), name="final",
        cost_estimate=pl.CostEstimate(flops=1 << 34, bytes_accessed=1 << 25, transcendentals=0),
    )(turn, q_in, k_in, inv_q, inv_k, got)
    return (d_q, d_k, d_v, part[0:SHARD], part[64:64 + SHARD])


def solution(mesh):
    rows = P(("dp", "seq"), None)
    return jax.shard_map(
        local, mesh=mesh,
        in_specs=(rows, rows, rows, P("dp"), P("dp"), P("dp", None)),
        out_specs=(rows, rows, rows, P("dp"), P("dp")), check_vma=False)
```
